256 devices in a mesh: expert: 16 (over x, y_hi, core), tensor: 8 (over z), dp: 2 (over y_lo).
Axes of the slice: x: 4, y: 4 (y_hi: 2, y_lo: 2; y = y_hi * 2 + y_lo), z: 8, core: 2. Of those that a mesh axis runs over, the one named last changes fastest.
Arguments:
- tokens: bfloat16 [8192, 3072], P(('expert', 'dp'), 'tensor'), may hold values from -6 to 6
- out_grad: bfloat16 [8192, 3072], P(('expert', 'dp'), 'tensor'), may hold values from -6 to 6
- gate_weight: bfloat16 [5376, 3072], P('expert', 'tensor'), may hold values from -0.109375 to 0.109375
- up_weight: bfloat16 [5376, 3072], P('expert', 'tensor'), may hold values from -0.109375 to 0.109375
- down_weight: bfloat16 [5376, 3072], P('expert', 'tensor'), may hold values from -0.078125 to 0.078125
- route_count: int32 [32], P(('expert', 'dp')), may hold values from 24 to 96, as said below
- route_index: int32 [3072], P(('expert', 'dp')), may hold values from 0 to 255, as said below
- route_gate: float32 [3072], P(('expert', 'dp')), may hold values from 0.1 to 1
Outputs:
- mixed: bfloat16 [8192, 3072], P(('expert', 'dp'), 'tensor')
- input_grad: bfloat16 [8192, 3072], P(('expert', 'dp'), 'tensor')
- grad_gate: float32 [5376, 3072], P('expert', ('tensor', 'dp'))
- grad_up: float32 [5376, 3072], P('expert', ('tensor', 'dp'))
- grad_down: float32 [5376, 3072], P('expert', ('tensor', 'dp'))
The draws below stay inside these ranges and needn't reach their ends.
Inputs may be any that keep to these rules, and one draw needn't show every extreme that they name: `route_count`: one shard's count is exactly 96 and another's exactly 24. `route_index`: within one shard's 96 slots the token indices are distinct.
All inputs are finite; a program needn't handle non-finite values.
Results may differ from the reference program's by a relative error of at most 0.035.
Values may be sent and summed in bfloat16 or wider, within the bound.
No kernel may reach another device: no remote copies, remote signals or barrier semaphores. Data moves between devices by JAX's collectives and lax.ppermute only.
A program may use at most 64 MiB of HBM per device.

```python
import jax
import jax.numpy as jnp
from jax import lax

D = 3072
FF = 5376
TOK_DEV = 256
CAP = 96
GROUPS = 32
TOKENS = 8192
SLOTS = 3072
N_EXPERT = 16
N_DP = 2


def draw_route_count(key, part):
    key = jax.random.fold_in(key, 1)
    key_count, key_full, key_least = jax.random.split(key, 3)
    counts = jax.random.randint(key_count, (GROUPS,), CAP // 4, CAP + 1)
    fullest = jax.random.randint(key_full, (), 0, GROUPS)
    least = (fullest + 1 + jax.random.randint(key_least, (), 0, GROUPS - 1)) % GROUPS
    position = jnp.arange(GROUPS)
    counts = jnp.where(position == fullest, CAP, jnp.where(position == least, CAP // 4, counts))
    return counts.astype(jnp.int32)


def draw_route_index(key, part):
    key = jax.random.fold_in(key, 2)
    subkeys = jax.random.split(key, GROUPS)
    chosen = jax.vmap(lambda subkey: jax.random.permutation(subkey, TOK_DEV)[:CAP])(subkeys)
    return chosen.reshape(-1).astype(jnp.int32)


def level_of(stream_key, extent, cuts, low, largest):
    factor_of, own = 1.0, jax.random.fold_in(stream_key, 6)
    for dim, parts in cuts:
        draws = jnp.exp(jax.random.uniform(jax.random.fold_in(own, dim), (parts,), jnp.float32, low / len(cuts), largest / len(cuts)))
        factor_of = factor_of * jnp.repeat(draws, extent[dim] // parts).reshape([-1 if axis == dim else 1 for axis in range(len(extent))])
    return factor_of


def scatter_about(rng, extent, spread, reach, shards=(), kind=jnp.bfloat16):
    loudness = level_of(rng, extent, shards, -0.22, 0.18) if shards else 1.0
    entries = jax.random.normal(rng, extent, jnp.float32) * spread * loudness
    return jnp.minimum(jnp.maximum(entries, -reach), reach).astype(kind)


def setup_inputs(seed: int = 0) -> dict:
    key_list = jax.random.split(jax.random.key(seed), 9)
    tokens = scatter_about(key_list[0], (TOKENS, D), 1.0, 6.0, ((0, 32), (1, 8)))
    out_grad = scatter_about(key_list[1], (TOKENS, D), 1.0, 6.0, ((0, 32), (1, 8)))
    gate_weight = scatter_about(key_list[2], (FF, D), D ** -0.5, 0.109375, ((0, 16), (1, 8)))
    up_weight = scatter_about(key_list[3], (FF, D), D ** -0.5, 0.109375, ((0, 16), (1, 8)))
    down_weight = scatter_about(key_list[4], (FF, D), FF ** -0.5, 0.078125, ((0, 16), (1, 8)))
    route_count = draw_route_count(jax.random.fold_in(key_list[8], 71), 0)
    route_index = draw_route_index(jax.random.fold_in(key_list[8], 71), 0)
    route_gate = jnp.clip(0.1 + 0.9 * jax.random.uniform(key_list[7], (SLOTS,), jnp.float32) ** level_of(key_list[7], (SLOTS,), ((0, 32),), -0.2, 0.2), 0.1, 1.0)
    return {"tokens": tokens, "out_grad": out_grad, "gate_weight": gate_weight, "up_weight": up_weight, "down_weight": down_weight, "route_count": route_count, "route_index": route_index, "route_gate": route_gate}


def contract_features(left, right):
    return lax.dot_general(left, right, (((1,), (1,)), ((), ())), preferred_element_type=jnp.float32)


def one_group(operands, gate_weight, up_weight, down_weight):
    token_rows, grad_block, index, route_weight, is_live = operands
    rows = jnp.take(token_rows, index, axis=0)
    grad_rows = (route_weight[:, None] * jnp.take(grad_block, index, axis=0).astype(jnp.float32)).astype(jnp.bfloat16)
    gate_pre = contract_features(rows, gate_weight)
    up_pre = contract_features(rows, up_weight)
    sigmoid_gate = jax.nn.sigmoid(gate_pre)
    activated = gate_pre * sigmoid_gate
    hidden = (activated * up_pre).astype(jnp.bfloat16)
    out_rows = jnp.dot(hidden, down_weight, preferred_element_type=jnp.float32)
    d_hidden = contract_features(grad_rows, down_weight)
    d_gate = (d_hidden * up_pre * sigmoid_gate * (1.0 + gate_pre * (1.0 - sigmoid_gate))).astype(jnp.bfloat16)
    d_up = (d_hidden * activated).astype(jnp.bfloat16)
    back_rows = jnp.dot(d_gate, gate_weight, preferred_element_type=jnp.float32) + jnp.dot(d_up, up_weight, preferred_element_type=jnp.float32)
    mixed = jnp.zeros((TOK_DEV, D), jnp.float32).at[index].add(route_weight[:, None] * out_rows)
    back = jnp.zeros((TOK_DEV, D), jnp.float32).at[index].add(jnp.where(is_live[:, None], back_rows, 0.0))
    return mixed.astype(jnp.bfloat16), back.astype(jnp.bfloat16), rows, grad_rows, hidden, d_gate, d_up


def reference(tokens, out_grad, gate_weight, up_weight, down_weight, route_count, route_index, route_gate):
    groups = N_EXPERT * N_DP
    token_blocks = tokens.reshape(groups, TOK_DEV, D)
    grad_blocks = out_grad.reshape(groups, TOK_DEV, D)
    index_blocks = route_index.reshape(groups, CAP).astype(jnp.int32)
    is_live = jnp.arange(CAP, dtype=jnp.int32)[None, :] < route_count[:, None]
    route_weight = jnp.where(is_live, route_gate.reshape(groups, CAP), 0.0).astype(jnp.float32)
    results = lax.map(lambda operands: one_group(operands, gate_weight, up_weight, down_weight), (token_blocks, grad_blocks, index_blocks, route_weight, is_live))
    mixed, back, rows, grad_rows, hidden, d_gate, d_up = results
    block = FF // N_EXPERT
    rows_four = rows.reshape(N_EXPERT, N_DP, CAP, D)
    grads_four = grad_rows.reshape(N_EXPERT, N_DP, CAP, D)
    hidden_five = hidden.reshape(N_EXPERT, N_DP, CAP, N_EXPERT, block)
    dgate_five = d_gate.reshape(N_EXPERT, N_DP, CAP, N_EXPERT, block)
    dup_five = d_up.reshape(N_EXPERT, N_DP, CAP, N_EXPERT, block)
    home_ids = jnp.arange(N_EXPERT, dtype=jnp.int32)

    def cycle_step(accums, step):
        position = (home_ids + step) % N_EXPERT
        sel_rows = rows_four[position].astype(jnp.float32)
        sel_grads = grads_four[position].astype(jnp.float32)
        sel_hidden = hidden_five[position, :, :, home_ids, :].astype(jnp.float32)
        sel_dgate = dgate_five[position, :, :, home_ids, :].astype(jnp.float32)
        sel_dup = dup_five[position, :, :, home_ids, :].astype(jnp.float32)
        term_gate = jnp.einsum("hdrf,hdrc->hdfc", sel_dgate, sel_rows)
        term_up = jnp.einsum("hdrf,hdrc->hdfc", sel_dup, sel_rows)
        term_down = jnp.einsum("hdrf,hdrc->hdfc", sel_hidden, sel_grads)
        new_gate = (accums[0].astype(jnp.float32) + term_gate).astype(jnp.bfloat16)
        new_up = (accums[1].astype(jnp.float32) + term_up).astype(jnp.bfloat16)
        new_down = (accums[2].astype(jnp.float32) + term_down).astype(jnp.bfloat16)
        return (new_gate, new_up, new_down), None

    zeros = jnp.zeros((N_EXPERT, N_DP, block, D), jnp.bfloat16)
    accums, unused = lax.scan(cycle_step, (zeros, zeros, zeros), jnp.arange(N_EXPERT, dtype=jnp.int32))
    grad_gate = jnp.sum(accums[0].astype(jnp.float32), axis=1).reshape(FF, D)
    grad_up = jnp.sum(accums[1].astype(jnp.float32), axis=1).reshape(FF, D)
    grad_down = jnp.sum(accums[2].astype(jnp.float32), axis=1).reshape(FF, D)
    return mixed.reshape(TOKENS, D), back.reshape(TOKENS, D), grad_gate, grad_up, grad_down
```

```python
import jax
import jax.numpy as jnp
from jax import lax
from jax.sharding import PartitionSpec as P

BF16 = jnp.bfloat16
F32 = jnp.float32


def dot(left, right, left_dim, right_dim):
    return lax.dot_general(
        left, right, (((left_dim,), (right_dim,)), ((), ())), preferred_element_type=F32
    )


def on_device(
    tokens, out_grad, gate_weight, up_weight, down_weight, route_count, route_index, route_gate
):
    capacity = route_index.shape[0]
    token_count, width = tokens.shape
    block = gate_weight.shape[0]
    is_live = jnp.arange(capacity, dtype=jnp.int32) < route_count[0]
    route_weight = jnp.where(is_live, route_gate, 0.0)
    pick = (
        route_index[:, None] == jnp.arange(token_count, dtype=jnp.int32)[None, :]
    ).astype(BF16)
    rows_here = dot(pick, tokens, 1, 0).astype(BF16)
    grads_here = (route_weight[:, None] * dot(pick, out_grad, 1, 0)).astype(BF16)

    gathered = lax.all_gather(
        jnp.concatenate([rows_here, grads_here], axis=1), "expert", axis=0, tiled=True
    )
    rows, grads = gathered[:, :width], gathered[:, width:]

    pre = jnp.concatenate(
        [
            dot(rows, gate_weight, 1, 1).astype(BF16),
            dot(rows, up_weight, 1, 1).astype(BF16),
            dot(grads, down_weight, 1, 1).astype(BF16),
        ],
        axis=1,
    )
    sums = lax.psum_scatter(pre, "tensor", scatter_dimension=0, tiled=True).astype(F32)
    gate_pre, up_pre, d_hidden = sums[:, :block], sums[:, block : 2 * block], sums[:, 2 * block :]
    sigmoid_gate = jax.nn.sigmoid(gate_pre)
    activated = gate_pre * sigmoid_gate
    hidden = (activated * up_pre).astype(BF16)
    d_gate = (d_hidden * up_pre * sigmoid_gate * (1.0 + gate_pre * (1.0 - sigmoid_gate))).astype(
        BF16
    )
    d_up = (d_hidden * activated).astype(BF16)
    acts = lax.all_gather(
        jnp.concatenate([hidden, d_gate, d_up], axis=1), "tensor", axis=0, tiled=True
    )
    hidden, d_gate, d_up = acts[:, :block], acts[:, block : 2 * block], acts[:, 2 * block :]

    out_part = dot(hidden, down_weight, 1, 0)
    back_part = dot(d_gate, gate_weight, 1, 0) + dot(d_up, up_weight, 1, 0)
    mine = lax.psum_scatter(
        jnp.concatenate([out_part.astype(BF16), back_part.astype(BF16)], axis=1),
        "expert",
        scatter_dimension=0,
        tiled=True,
    ).astype(F32)
    out_rows = (route_weight[:, None] * mine[:, :width]).astype(BF16)
    back_rows = jnp.where(is_live[:, None], mine[:, width:], 0.0).astype(BF16)
    mixed = dot(pick, out_rows, 0, 0).astype(BF16)
    input_grad = dot(pick, back_rows, 0, 0).astype(BF16)

    grads_w = jnp.concatenate(
        [dot(d_gate, rows, 0, 0), dot(d_up, rows, 0, 0), dot(hidden, grads, 0, 0)], axis=0
    ).astype(BF16)
    half = width // 2
    first = lax.axis_index("dp") == 0
    low, high = grads_w[:, :half], grads_w[:, half:]
    got = lax.ppermute(jnp.where(first, high, low), "dp", [(0, 1), (1, 0)])
    total = jnp.where(first, low, high).astype(F32) + got.astype(F32)
    return (
        mixed,
        input_grad,
        total[:block],
        total[block : 2 * block],
        total[2 * block :],
    )


def solution(mesh):
    return jax.shard_map(
        on_device,
        mesh=mesh,
        in_specs=(
            P(("expert", "dp"), "tensor"),
            P(("expert", "dp"), "tensor"),
            P("expert", "tensor"),
            P("expert", "tensor"),
            P("expert", "tensor"),
            P(("expert", "dp")),
            P(("expert", "dp")),
            P(("expert", "dp")),
        ),
        out_specs=(
            P(("expert", "dp"), "tensor"),
            P(("expert", "dp"), "tensor"),
            P("expert", ("tensor", "dp")),
            P("expert", ("tensor", "dp")),
            P("expert", ("tensor", "dp")),
        ),
        check_vma=False,
    )
```

```python
import jax
import jax.numpy as jnp
from jax import lax
from jax.sharding import PartitionSpec as P

BF16 = jnp.bfloat16
F32 = jnp.float32
XS, YS, CORES, RING = 4, 2, 2, 8
CHIPS = XS * YS


def dot(left, right, left_dim, right_dim):
    return lax.dot_general(
        left, right, (((left_dim,), (right_dim,)), ((), ())), preferred_element_type=F32
    )


def core_swap(x):
    return lax.ppermute(x, "expert", [(e, e ^ 1) for e in range(CHIPS * CORES)])


def chip_pairs(delta):
    pairs = []
    for e in range(CHIPS * CORES):
        x, y, core = e // 4, (e // 2) % 2, e % 2
        for z in range(RING):
            j = (z + delta) % RING
            owner = (((x + j // YS) % XS) * YS + (y + j % YS) % YS) * CORES + core
            pairs.append((e * RING + z, owner * RING + z))
    return pairs


def from_owner(x, delta):
    return lax.ppermute(x, ("expert", "tensor"), [(o, r) for r, o in chip_pairs(delta)])


def to_owner(x, delta):
    return lax.ppermute(x, ("expert", "tensor"), chip_pairs(delta))


def ring(x, by):
    return lax.ppermute(x, "tensor", [(z, (z + by) % RING) for z in range(RING)])


def on_device(
    tokens, out_grad, gate_weight, up_weight, down_weight, route_count, route_index, route_gate
):
    capacity = route_index.shape[0]
    token_count, width = tokens.shape
    block = gate_weight.shape[0]
    core0 = lax.axis_index("expert") % 2 == 0
    dp0 = lax.axis_index("dp") == 0
    is_live = jnp.arange(capacity, dtype=jnp.int32) < route_count[0]
    route_weight = jnp.where(is_live, route_gate, 0.0)
    pick = (
        route_index[:, None] == jnp.arange(token_count, dtype=jnp.int32)[None, :]
    ).astype(BF16)
    rows_here = dot(pick, tokens, 1, 0).astype(BF16)
    grads_here = (route_weight[:, None] * dot(pick, out_grad, 1, 0)).astype(BF16)

    nothing = jnp.zeros_like(gate_weight)
    w_in = jnp.concatenate(
        [
            jnp.concatenate([gate_weight, nothing], axis=1),
            jnp.concatenate([up_weight, nothing], axis=1),
            jnp.concatenate([nothing, down_weight], axis=1),
        ],
        axis=0,
    )
    w_out = jnp.concatenate(
        [
            jnp.concatenate([down_weight, nothing], axis=1),
            jnp.concatenate([nothing, gate_weight], axis=1),
            jnp.concatenate([nothing, up_weight], axis=1),
        ],
        axis=0,
    )

    mine = jnp.where(core0, rows_here, grads_here)
    got = core_swap(jnp.where(core0, grads_here, rows_here))
    piece = jnp.where(
        core0, jnp.concatenate([mine, got], axis=0), jnp.concatenate([got, mine], axis=0)
    )
    payload = {}
    for delta in (4, 3, 5, 2, 6, 1, 7, 0):
        came = from_owner(piece, delta)
        other = core_swap(came)
        payload[delta] = jnp.concatenate(
            [jnp.where(core0, came, other), jnp.where(core0, other, came)], axis=1
        )

    pre = {delta: dot(payload[delta], w_in, 1, 1) for delta in payload}

    def half(delta, h):
        return pre[delta][h * capacity : (h + 1) * capacity]

    sums = []
    for h in range(2):
        left_path = (4, 5, 6, 7) if h == 0 else (5, 6, 7)
        right_path = (3, 2, 1) if h == 0 else (4, 3, 2, 1)
        ends = []
        for path, by in ((left_path, -1), (right_path, 1)):
            moving = None
            for delta in path:
                total = half(delta, h)
                if moving is not None:
                    total = total + moving.astype(F32)
                moving = ring(total.astype(BF16), by)
            ends.append(moving.astype(F32))
        sums.append(half(0, h) + ends[0] + ends[1])

    acts_own = []
    for total in sums:
        gate_pre, up_pre, d_hidden = (
            total[:, :block],
            total[:, block : 2 * block],
            total[:, 2 * block :],
        )
        sigmoid_gate = jax.nn.sigmoid(gate_pre)
        activated = gate_pre * sigmoid_gate
        hidden = (activated * up_pre).astype(BF16)
        d_gate = (
            d_hidden * up_pre * sigmoid_gate * (1.0 + gate_pre * (1.0 - sigmoid_gate))
        ).astype(BF16)
        d_up = (d_hidden * activated).astype(BF16)
        acts_own.append(jnp.concatenate([hidden, d_gate, d_up], axis=1))

    halves = {0: acts_own}
    right = list(acts_own)
    left = list(acts_own)
    for step in (1, 2, 3):
        right = [ring(a, 1) for a in right]
        left = [ring(a, -1) for a in left]
        halves[RING - step] = right
        halves[step] = left
    halves[4] = [ring(right[0], 1), ring(left[1], -1)]
    acts = {delta: jnp.concatenate(halves[delta], axis=0) for delta in halves}

    arrived = []
    for delta in (0, 7, 1, 6, 2, 5, 3, 4):
        part = dot(acts[delta], w_out, 1, 0)
        low, high = part[:capacity], part[capacity:]
        swapped = core_swap(jnp.where(core0, high, low).astype(BF16))
        pair_sum = jnp.where(core0, low, high) + swapped.astype(F32)
        arrived.append(to_owner(pair_sum.astype(BF16), delta))
    total = arrived[0].astype(F32)
    for came in arrived[1:]:
        total = total + came.astype(F32)
    out_rows = (route_weight[:, None] * total[:, :width]).astype(BF16)
    back_rows = jnp.where(is_live[:, None], total[:, width:], 0.0).astype(BF16)
    mixed = dot(pick, out_rows, 0, 0).astype(BF16)
    input_grad = dot(pick, back_rows, 0, 0).astype(BF16)

    all_acts = jnp.concatenate([acts[delta] for delta in range(RING)], axis=0)
    all_payload = jnp.concatenate([payload[delta] for delta in range(RING)], axis=0)
    by_rows = dot(all_payload[:, :width], all_acts, 0, 0)
    by_grads = dot(all_payload[:, width:], all_acts, 0, 0)
    unit = lax.broadcasted_iota(jnp.int32, by_rows.shape, 1)
    grads_w = jnp.where(unit < block, by_grads, by_rows)
    part = width // 2
    low, high = grads_w[:part], grads_w[part:]
    got = lax.ppermute(jnp.where(dp0, high, low).astype(BF16), "dp", [(0, 1), (1, 0)])
    grads_w = jnp.where(dp0, low, high) + got.astype(F32)
    return (
        mixed,
        input_grad,
        grads_w[:, block : 2 * block].T,
        grads_w[:, 2 * block :].T,
        grads_w[:, :block].T,
    )


def solution(mesh):
    return jax.shard_map(
        on_device,
        mesh=mesh,
        in_specs=(
            P(("expert", "dp"), "tensor"),
            P(("expert", "dp"), "tensor"),
            P("expert", "tensor"),
            P("expert", "tensor"),
            P("expert", "tensor"),
            P(("expert", "dp")),
            P(("expert", "dp")),
            P(("expert", "dp")),
        ),
        out_specs=(
            P(("expert", "dp"), "tensor"),
            P(("expert", "dp"), "tensor"),
            P("expert", ("tensor", "dp")),
            P("expert", ("tensor", "dp")),
            P("expert", ("tensor", "dp")),
        ),
        check_vma=False,
    )
```

```python
import jax
import jax.numpy as jnp
from jax import lax
from jax.sharding import Mesh
from jax.sharding import PartitionSpec as P

BF16 = jnp.bfloat16
F32 = jnp.float32
XS, YS, CORES, RING = 4, 2, 2, 8
CHIPS = XS * YS


def dot(left, right, left_dim, right_dim):
    return lax.dot_general(
        left, right, (((left_dim,), (right_dim,)), ((), ())), preferred_element_type=F32
    )


def core_swap(x):
    return lax.ppermute(x, "core", [(0, 1), (1, 0)])


def among_chips(x):
    return lax.all_to_all(x, ("x", "y"), 0, 0, tiled=True)


def ring(x, by):
    return lax.ppermute(x, "tensor", [(z, (z + by) % RING) for z in range(RING)])


def on_device(
    tokens, out_grad, gate_weight, up_weight, down_weight, route_count, route_index, route_gate
):
    capacity = route_index.shape[0]
    token_count, width = tokens.shape
    block = gate_weight.shape[0]
    core0 = lax.axis_index("core") == 0
    here = lax.axis_index("tensor")
    dp0 = lax.axis_index("dp") == 0
    is_live = jnp.arange(capacity, dtype=jnp.int32) < route_count[0]
    route_weight = jnp.where(is_live, route_gate, 0.0)
    pick = (
        route_index[:, None] == jnp.arange(token_count, dtype=jnp.int32)[None, :]
    ).astype(BF16)
    rows_here = dot(pick, tokens, 1, 0).astype(BF16)
    grads_here = (route_weight[:, None] * dot(pick, out_grad, 1, 0)).astype(BF16)

    nothing = jnp.zeros_like(gate_weight)
    w_in = jnp.concatenate(
        [
            jnp.concatenate([gate_weight, nothing], axis=1),
            jnp.concatenate([up_weight, nothing], axis=1),
            jnp.concatenate([nothing, down_weight], axis=1),
        ],
        axis=0,
    )
    w_out = jnp.concatenate(
        [
            jnp.concatenate([down_weight, nothing], axis=1),
            jnp.concatenate([nothing, gate_weight], axis=1),
            jnp.concatenate([nothing, up_weight], axis=1),
        ],
        axis=0,
    )

    mine = jnp.where(core0, rows_here, grads_here)
    got = core_swap(jnp.where(core0, grads_here, rows_here))
    piece = jnp.where(
        core0, jnp.concatenate([mine, got], axis=0), jnp.concatenate([got, mine], axis=0)
    )
    came = among_chips(jnp.broadcast_to(piece[None], (CHIPS,) + piece.shape))
    other = core_swap(came)
    rows_all = jnp.where(core0, came, other)
    grads_all = jnp.where(core0, other, came)
    payload = {}
    for delta in range(RING):
        at = (here + delta) % RING
        payload[delta] = jnp.concatenate(
            [
                lax.dynamic_index_in_dim(rows_all, at, 0, keepdims=False),
                lax.dynamic_index_in_dim(grads_all, at, 0, keepdims=False),
            ],
            axis=1,
        )

    pre = {delta: dot(payload[delta], w_in, 1, 1) for delta in payload}

    def half(delta, h):
        return pre[delta][h * capacity : (h + 1) * capacity]

    sums = []
    for h in range(2):
        left_path = (4, 5, 6, 7) if h == 0 else (5, 6, 7)
        right_path = (3, 2, 1) if h == 0 else (4, 3, 2, 1)
        ends = []
        for path, by in ((left_path, -1), (right_path, 1)):
            moving = None
            for delta in path:
                total = half(delta, h)
                if moving is not None:
                    total = total + moving.astype(F32)
                moving = ring(total.astype(BF16), by)
            ends.append(moving.astype(F32))
        sums.append(half(0, h) + ends[0] + ends[1])

    acts_own = []
    for total in sums:
        gate_pre, up_pre, d_hidden = (
            total[:, :block],
            total[:, block : 2 * block],
            total[:, 2 * block :],
        )
        sigmoid_gate = jax.nn.sigmoid(gate_pre)
        activated = gate_pre * sigmoid_gate
        hidden = (activated * up_pre).astype(BF16)
        d_gate = (
            d_hidden * up_pre * sigmoid_gate * (1.0 + gate_pre * (1.0 - sigmoid_gate))
        ).astype(BF16)
        d_up = (d_hidden * activated).astype(BF16)
        acts_own.append(jnp.concatenate([hidden, d_gate, d_up], axis=1))

    halves = {0: acts_own}
    right = list(acts_own)
    left = list(acts_own)
    for step in (1, 2, 3):
        right = [ring(a, 1) for a in right]
        left = [ring(a, -1) for a in left]
        halves[RING - step] = right
        halves[step] = left
    halves[4] = [ring(right[0], 1), ring(left[1], -1)]
    acts = {delta: jnp.concatenate(halves[delta], axis=0) for delta in halves}

    by_chip = jnp.zeros((CHIPS, capacity, 2 * width), BF16)
    for group in ((0, 7, 1, 6, 2), (5, 3, 4)):
        parts = [dot(acts[delta], w_out, 1, 0) for delta in group]
        keep = [jnp.where(core0, p[:capacity], p[capacity:]) for p in parts]
        give = [jnp.where(core0, p[capacity:], p[:capacity]).astype(BF16) for p in parts]
        swapped = core_swap(jnp.stack(give))
        for n, delta in enumerate(group):
            pair_sum = (keep[n] + swapped[n].astype(F32)).astype(BF16)
            by_chip = lax.dynamic_update_index_in_dim(
                by_chip, pair_sum, (here + delta) % RING, 0
            )
    all_acts = jnp.concatenate([acts[delta] for delta in range(RING)], axis=0)
    by_chip, all_acts = lax.optimization_barrier((by_chip, all_acts))
    total = jnp.sum(among_chips(by_chip).astype(F32), axis=0)
    out_rows = (route_weight[:, None] * total[:, :width]).astype(BF16)
    back_rows = jnp.where(is_live[:, None], total[:, width:], 0.0).astype(BF16)
    mixed = dot(pick, out_rows, 0, 0).astype(BF16)
    input_grad = dot(pick, back_rows, 0, 0).astype(BF16)

    all_payload = jnp.concatenate([payload[delta] for delta in range(RING)], axis=0)
    by_rows = dot(all_payload[:, :width], all_acts, 0, 0)
    by_grads = dot(all_payload[:, width:], all_acts, 0, 0)
    unit = lax.broadcasted_iota(jnp.int32, by_rows.shape, 1)
    grads_w = jnp.where(unit < block, by_grads, by_rows)
    part = width // 2
    low, high = grads_w[:part], grads_w[part:]
    got = lax.ppermute(jnp.where(dp0, high, low).astype(BF16), "dp", [(0, 1), (1, 0)])
    grads_w = jnp.where(dp0, low, high) + got.astype(F32)
    return (
        mixed,
        input_grad,
        grads_w[:, block : 2 * block].T,
        grads_w[:, 2 * block :].T,
        grads_w[:, :block].T,
    )


def solution(mesh):
    ways = (("x", "y", "core"), "tensor", "dp")
    chips = Mesh(mesh.devices.reshape(XS, YS, CORES, RING, 2), ways[0] + ways[1:])
    expert, tensor, dp = ways
    tokens = P(expert + (dp,), tensor)
    weight = P(expert, tensor)
    slots = P(expert + (dp,))
    grad = P(expert, (tensor, dp))
    return jax.shard_map(
        on_device,
        mesh=chips,
        in_specs=(tokens, tokens, weight, weight, weight, slots, slots, slots),
        out_specs=(tokens, tokens, grad, grad, grad),
        check_vma=False,
    )
```

```python
import functools

import jax
import jax.numpy as jnp
from jax import lax
from jax.experimental import pallas as pl
from jax.experimental.pallas import tpu as pltpu
from jax.sharding import Mesh
from jax.sharding import PartitionSpec as P

BF16 = jnp.bfloat16
F32 = jnp.float32
XS, YS, CORES, RING = 4, 2, 2, 8
CHIPS = XS * YS
VMEM_LIMIT = 40 * 1024 * 1024
WHOLE = pl.BlockSpec(memory_space=pltpu.VMEM)
SCALARS = pl.BlockSpec(memory_space=pltpu.SMEM)


def dot(left, right, left_dim, right_dim):
    return lax.dot_general(
        left, right, (((left_dim,), (right_dim,)), ((), ())), preferred_element_type=F32
    )


def core_swap(x):
    return lax.ppermute(x, "core", [(0, 1), (1, 0)])


def among_chips(x):
    return lax.all_to_all(x, ("x", "y"), 0, 0, tiled=True)


def ring(x, by):
    return lax.ppermute(x, "tensor", [(z, (z + by) % RING) for z in range(RING)])


def local_call(body, name, out_shape, operands):
    return pl.pallas_call(
        body,
        out_shape=out_shape,
        in_specs=[SCALARS] + [WHOLE] * len(operands[1:]),
        out_specs=jax.tree.map(lambda _: WHOLE, out_shape),
        compiler_params=pltpu.CompilerParams(vmem_limit_bytes=VMEM_LIMIT),
        cost_estimate=pl.CostEstimate(flops=1, bytes_accessed=1, transcendentals=0),
        name=name,
    )(*operands)


def pre_body(deltas, where_ref, came_ref, other_ref, w_ref, payload_ref, *pre_refs):
    here, core = where_ref[0], where_ref[1]
    w = w_ref[...]
    for n, delta in enumerate(deltas):
        at = lax.rem(here + delta, RING)
        came, other = came_ref[at], other_ref[at]
        rows = jnp.where(core == 0, came, other)
        grads = jnp.where(core == 0, other, came)
        x = jnp.concatenate([rows, grads], axis=1)
        payload_ref[n] = x
        pre_refs[n][...] = dot(x, w, 1, 1).astype(pre_refs[n].dtype)


def out_body(deltas, where_ref, w_ref, *refs):
    core = where_ref[1]
    keep_ref, give_ref = refs[-2:]
    w = w_ref[...]
    for n in range(len(deltas)):
        low = dot(refs[2 * n][...], w, 1, 0)
        high = dot(refs[2 * n + 1][...], w, 1, 0)
        keep_ref[n] = jnp.where(core == 0, low, high)
        give_ref[n] = jnp.where(core == 0, high, low).astype(BF16)


def sum_body(deltas, where_ref, keep_ref, got_ref, keep_last_ref, got_last_ref, out_ref):
    here = where_ref[0]
    for n, delta in enumerate(deltas):
        out_ref[lax.rem(here + delta, RING)] = (keep_ref[n] + got_ref[n].astype(F32)).astype(BF16)
    out_ref[lax.rem(here + RING // 2, RING)] = (
        keep_last_ref[0] + got_last_ref[0].astype(F32)
    ).astype(BF16)


def on_device(
    tokens, out_grad, gate_weight, up_weight, down_weight, route_count, route_index, route_gate
):
    capacity = route_index.shape[0]
    token_count, width = tokens.shape
    block = gate_weight.shape[0]
    units = 3 * block
    core = lax.axis_index("core")
    core0 = core == 0
    here = lax.axis_index("tensor")
    dp0 = lax.axis_index("dp") == 0
    where = jnp.stack([here, core]).astype(jnp.int32)
    is_live = jnp.arange(capacity, dtype=jnp.int32) < route_count[0]
    route_weight = jnp.where(is_live, route_gate, 0.0)
    pick = (
        route_index[:, None] == jnp.arange(token_count, dtype=jnp.int32)[None, :]
    ).astype(BF16)
    rows_here = dot(pick, tokens, 1, 0).astype(BF16)
    grads_here = (route_weight[:, None] * dot(pick, out_grad, 1, 0)).astype(BF16)

    nothing = jnp.zeros_like(gate_weight)
    w_in = jnp.concatenate(
        [
            jnp.concatenate([gate_weight, nothing], axis=1),
            jnp.concatenate([up_weight, nothing], axis=1),
            jnp.concatenate([nothing, down_weight], axis=1),
        ],
        axis=0,
    )
    w_out = jnp.concatenate(
        [
            jnp.concatenate([down_weight, nothing], axis=1),
            jnp.concatenate([nothing, gate_weight], axis=1),
            jnp.concatenate([nothing, up_weight], axis=1),
        ],
        axis=0,
    )

    mine = jnp.where(core0, rows_here, grads_here)
    got = core_swap(jnp.where(core0, grads_here, rows_here))
    piece = jnp.where(
        core0, jnp.concatenate([mine, got], axis=0), jnp.concatenate([got, mine], axis=0)
    )
    came = among_chips(jnp.broadcast_to(piece[None], (CHIPS,) + piece.shape))
    other = core_swap(came)
    pre = {}
    payloads = []
    first, rest = (4, 3, 5), (2, 6, 1, 7, 0)
    for deltas, name in ((first, "pre_first"), (rest, "pre_rest")):
        shapes = [jax.ShapeDtypeStruct((len(deltas), 2 * capacity, 2 * width), BF16)]
        for delta in deltas:
            shapes.append(
                jax.ShapeDtypeStruct((2 * capacity, units), BF16 if delta == 4 else F32)
            )
        payload, *blocks = local_call(
            functools.partial(pre_body, deltas), name, shapes, [where, came, other, w_in]
        )
        payloads.append(payload.reshape(-1, 2 * width))
        pre.update(zip(deltas, blocks))

    def half(delta, h):
        return pre[delta][h * capacity : (h + 1) * capacity]

    sums = []
    for h in range(2):
        left_path = (4, 5, 6, 7) if h == 0 else (5, 6, 7)
        right_path = (3, 2, 1) if h == 0 else (4, 3, 2, 1)
        ends = []
        for path, by in ((left_path, -1), (right_path, 1)):
            moving = None
            for delta in path:
                total = half(delta, h)
                if moving is not None:
                    total = total + moving.astype(F32)
                moving = ring(total.astype(BF16), by)
            ends.append(moving.astype(F32))
        sums.append(half(0, h) + ends[0] + ends[1])

    acts_own = []
    for total in sums:
        gate_pre, up_pre, d_hidden = (
            total[:, :block],
            total[:, block : 2 * block],
            total[:, 2 * block :],
        )
        sigmoid_gate = jax.nn.sigmoid(gate_pre)
        activated = gate_pre * sigmoid_gate
        hidden = (activated * up_pre).astype(BF16)
        d_gate = (
            d_hidden * up_pre * sigmoid_gate * (1.0 + gate_pre * (1.0 - sigmoid_gate))
        ).astype(BF16)
        d_up = (d_hidden * activated).astype(BF16)
        acts_own.append(jnp.concatenate([hidden, d_gate, d_up], axis=1))

    halves = {0: acts_own}
    right = list(acts_own)
    left = list(acts_own)
    for step in (1, 2, 3):
        right = [ring(a, 1) for a in right]
        left = [ring(a, -1) for a in left]
        halves[RING - step] = right
        halves[step] = left
    halves[4] = [ring(right[0], 1), ring(left[1], -1)]

    near, far = (0, 7, 1, 6, 2, 5, 3), (4,)
    kept, swapped = [], []
    for deltas, name in ((near, "out_near"), (far, "out_far")):
        shape = (len(deltas), capacity, 2 * width)
        keep, give = local_call(
            functools.partial(out_body, deltas),
            name,
            [jax.ShapeDtypeStruct(shape, F32), jax.ShapeDtypeStruct(shape, BF16)],
            [where, w_out] + [h for delta in deltas for h in halves[delta]],
        )
        kept.append(keep)
        swapped.append(core_swap(give))
    by_chip = local_call(
        functools.partial(sum_body, near),
        "pair_sum",
        jax.ShapeDtypeStruct((CHIPS, capacity, 2 * width), BF16),
        [where, kept[0], swapped[0], kept[1], swapped[1]],
    )
    all_acts = jnp.concatenate([h for delta in first + rest for h in halves[delta]], axis=0)
    by_chip, all_acts = lax.optimization_barrier((by_chip, all_acts))
    total = jnp.sum(among_chips(by_chip).astype(F32), axis=0)
    out_rows = (route_weight[:, None] * total[:, :width]).astype(BF16)
    back_rows = jnp.where(is_live[:, None], total[:, width:], 0.0).astype(BF16)
    mixed = dot(pick, out_rows, 0, 0).astype(BF16)
    input_grad = dot(pick, back_rows, 0, 0).astype(BF16)

    all_payload = jnp.concatenate(payloads, axis=0)
    by_rows = dot(all_payload[:, :width], all_acts, 0, 0)
    by_grads = dot(all_payload[:, width:], all_acts, 0, 0)
    unit = lax.broadcasted_iota(jnp.int32, by_rows.shape, 1)
    grads_w = jnp.where(unit < block, by_grads, by_rows)
    part = width // 2
    low, high = grads_w[:part], grads_w[part:]
    got = lax.ppermute(jnp.where(dp0, high, low).astype(BF16), "dp", [(0, 1), (1, 0)])
    grads_w = jnp.where(dp0, low, high) + got.astype(F32)
    return (
        mixed,
        input_grad,
        grads_w[:, block : 2 * block].T,
        grads_w[:, 2 * block :].T,
        grads_w[:, :block].T,
    )


def solution(mesh):
    ways = (("x", "y", "core"), "tensor", "dp")
    chips = Mesh(mesh.devices.reshape(XS, YS, CORES, RING, 2), ways[0] + ways[1:])
    expert, tensor, dp = ways
    tokens = P(expert + (dp,), tensor)
    weight = P(expert, tensor)
    slots = P(expert + (dp,))
    grad = P(expert, (tensor, dp))
    return jax.shard_map(
        on_device,
        mesh=chips,
        in_specs=(tokens, tokens, weight, weight, weight, slots, slots, slots),
        out_specs=(tokens, tokens, grad, grad, grad),
        check_vma=False,
    )
```

```python
import functools

import jax
import jax.numpy as jnp
from jax import lax
from jax.experimental import pallas as pl
from jax.experimental.pallas import tpu as pltpu
from jax.sharding import Mesh
from jax.sharding import PartitionSpec as P

BF16 = jnp.bfloat16
F32 = jnp.float32
XS, YS, CORES, RING = 4, 2, 2, 8
CHIPS = XS * YS
FIRST, LAST = 640, 768
VMEM_LIMIT = 40 * 1024 * 1024
WHOLE = pl.BlockSpec(memory_space=pltpu.VMEM)
SCALARS = pl.BlockSpec(memory_space=pltpu.SMEM)


def dot(left, right, left_dim, right_dim):
    return lax.dot_general(
        left, right, (((left_dim,), (right_dim,)), ((), ())), preferred_element_type=F32
    )


def core_swap(x):
    return lax.ppermute(x, "core", [(0, 1), (1, 0)])


def among_chips(x):
    return lax.all_to_all(x, ("x", "y"), 0, 0, tiled=True)


def ring(x, by):
    return lax.ppermute(x, "tensor", [(z, (z + by) % RING) for z in range(RING)])


def local_call(body, name, out_shape, operands, scratch=()):
    return pl.pallas_call(
        body,
        out_shape=out_shape,
        in_specs=[SCALARS] + [WHOLE] * len(operands[1:]),
        out_specs=jax.tree.map(lambda _: WHOLE, out_shape),
        scratch_shapes=scratch,
        compiler_params=pltpu.CompilerParams(vmem_limit_bytes=VMEM_LIMIT),
        cost_estimate=pl.CostEstimate(flops=1, bytes_accessed=1, transcendentals=0),
        name=name,
    )(*operands)


def pre_body(deltas, where_ref, came_ref, other_ref, w_rows_ref, w_grads_ref, payload_ref, *refs):
    here, core = where_ref[0], where_ref[1]
    width = came_ref.shape[-1]
    w_rows, w_grads = w_rows_ref[...], w_grads_ref[...]
    for n, delta in enumerate(deltas):
        at = lax.rem(here + delta, RING)
        came, other = came_ref[at], other_ref[at]
        rows = jnp.where(core == 0, came, other)
        grads = jnp.where(core == 0, other, came)
        payload_ref[n, :, :width] = rows
        payload_ref[n, :, width:] = grads
        a, b = dot(rows, w_rows, 1, 1), dot(grads, w_grads, 1, 1)
        kind = refs[n].dtype
        refs[n][:, :FIRST] = a[:, :FIRST].astype(kind)
        refs[n][:, FIRST:LAST] = (a[:, FIRST:] + b[:, : LAST - FIRST]).astype(kind)
        refs[n][:, LAST:] = b[:, LAST - FIRST :].astype(kind)


def join(refs, to_ref):
    size = refs[0].shape[0]
    for n, ref in enumerate(refs):
        to_ref[n * size : (n + 1) * size, :] = ref[...]


def out_body(deltas, where_ref, w_rows_ref, w_grads_ref, *refs):
    core = where_ref[1]
    keep_ref, give_ref, acts_ref = refs[-3:]
    join(refs[:-3], acts_ref)
    size, width = refs[0].shape[0], w_rows_ref.shape[1]
    out = dot(acts_ref[:, FIRST:], w_grads_ref[...], 1, 0)
    back = dot(acts_ref[:, :LAST], w_rows_ref[...], 1, 0)
    for n in range(len(deltas)):
        for cols, part in ((slice(0, width), out), (slice(width, 2 * width), back)):
            low = part[2 * n * size : (2 * n + 1) * size]
            high = part[(2 * n + 1) * size : (2 * n + 2) * size]
            keep_ref[n, :, cols] = jnp.where(core == 0, low, high)
            give_ref[n, :, cols] = jnp.where(core == 0, high, low).astype(BF16)


def weight_body(block, where_ref, first_ref, rest_ref, *refs):
    dp = where_ref[2]
    keep_ref, give_ref, acts_ref = refs[-3:]
    join(refs[:-3], acts_ref)
    part = keep_ref.shape[0]
    split = first_ref.shape[0]
    width = 2 * part

    def product(cols, units):
        return dot(first_ref[:, cols], acts_ref[:split, units], 0, 0) + dot(
            rest_ref[:, cols], acts_ref[split:, units], 0, 0
        )

    by_rows = product(slice(0, width), slice(0, LAST))
    by_grads = product(slice(width, 2 * width), slice(FIRST, acts_ref.shape[1]))
    unit = FIRST + lax.broadcasted_iota(jnp.int32, (part, LAST - FIRST), 1)
    for cols in (slice(0, FIRST), slice(FIRST, LAST), slice(LAST, acts_ref.shape[1])):
        halves = []
        for rows in (slice(0, part), slice(part, width)):
            if cols.stop == FIRST:
                halves.append(by_rows[rows, :FIRST])
            elif cols.start == FIRST:
                halves.append(
                    jnp.where(
                        unit < 2 * block, by_rows[rows, FIRST:], by_grads[rows, : LAST - FIRST]
                    )
                )
            else:
                halves.append(by_grads[rows, LAST - FIRST :])
        keep_ref[:, cols] = jnp.where(dp == 0, halves[0], halves[1])
        give_ref[:, cols] = jnp.where(dp == 0, halves[1], halves[0]).astype(BF16)


def scatter_body(where_ref, came_ref, index_ref, weight_ref, live_ref, mixed_ref, grad_ref):
    total = came_ref[0].astype(F32)
    for n in range(1, CHIPS):
        total = total + came_ref[n].astype(F32)
    token_count, width = mixed_ref.shape
    out_rows = (weight_ref[...] * total[:, :width]).astype(BF16)
    back_rows = jnp.where(live_ref[...] > 0, total[:, width:], 0.0).astype(BF16)
    token = lax.broadcasted_iota(jnp.int32, (token_count, index_ref.shape[1]), 0)
    place = jnp.where(token == index_ref[...], 1.0, 0.0).astype(BF16)
    mixed_ref[...] = dot(place, out_rows, 1, 0).astype(BF16)
    grad_ref[...] = dot(place, back_rows, 1, 0).astype(BF16)


def sum_body(deltas, where_ref, keep_ref, got_ref, keep_last_ref, got_last_ref, out_ref):
    here = where_ref[0]
    for n, delta in enumerate(deltas):
        out_ref[lax.rem(here + delta, RING)] = (keep_ref[n] + got_ref[n].astype(F32)).astype(BF16)
    out_ref[lax.rem(here + RING // 2, RING)] = (
        keep_last_ref[0] + got_last_ref[0].astype(F32)
    ).astype(BF16)


def on_device(
    tokens, out_grad, gate_weight, up_weight, down_weight, route_count, route_index, route_gate
):
    capacity = route_index.shape[0]
    token_count, width = tokens.shape
    block = gate_weight.shape[0]
    units = 3 * block
    core = lax.axis_index("core")
    core0 = core == 0
    here = lax.axis_index("tensor")
    where = jnp.stack([here, core, lax.axis_index("dp")]).astype(jnp.int32)
    is_live = jnp.arange(capacity, dtype=jnp.int32) < route_count[0]
    route_weight = jnp.where(is_live, route_gate, 0.0)
    pick = (
        route_index[:, None] == jnp.arange(token_count, dtype=jnp.int32)[None, :]
    ).astype(BF16)
    rows_here = dot(pick, tokens, 1, 0).astype(BF16)
    grads_here = (route_weight[:, None] * dot(pick, out_grad, 1, 0)).astype(BF16)

    w_rows = jnp.concatenate(
        [gate_weight, up_weight, jnp.zeros((LAST - 2 * block, width), BF16)], axis=0
    )
    w_grads = jnp.concatenate(
        [jnp.zeros((2 * block - FIRST, width), BF16), down_weight], axis=0
    )

    mine = jnp.where(core0, rows_here, grads_here)
    got = core_swap(jnp.where(core0, grads_here, rows_here))
    piece = jnp.where(
        core0, jnp.concatenate([mine, got], axis=0), jnp.concatenate([got, mine], axis=0)
    )
    came = among_chips(jnp.broadcast_to(piece[None], (CHIPS,) + piece.shape))
    other = core_swap(came)
    pre = {}
    payloads = []
    first, rest = (4, 3, 5), (2, 6, 1, 7, 0)
    for deltas, name in ((first, "pre_first"), (rest, "pre_rest")):
        shapes = [jax.ShapeDtypeStruct((len(deltas), 2 * capacity, 2 * width), BF16)]
        for delta in deltas:
            shapes.append(
                jax.ShapeDtypeStruct((2 * capacity, units), BF16 if delta == 4 else F32)
            )
        payload, *blocks = local_call(
            functools.partial(pre_body, deltas), name, shapes, [where, came, other, w_rows, w_grads]
        )
        payloads.append(payload.reshape(-1, 2 * width))
        pre.update(zip(deltas, blocks))

    def half(delta, h):
        return pre[delta][h * capacity : (h + 1) * capacity]

    sums = []
    for h in range(2):
        left_path = (4, 5, 6, 7) if h == 0 else (5, 6, 7)
        right_path = (3, 2, 1) if h == 0 else (4, 3, 2, 1)
        ends = []
        for path, by in ((left_path, -1), (right_path, 1)):
            moving = None
            for delta in path:
                total = half(delta, h)
                if moving is not None:
                    total = total + moving.astype(F32)
                moving = ring(total.astype(BF16), by)
            ends.append(moving.astype(F32))
        sums.append(half(0, h) + ends[0] + ends[1])

    acts_own = []
    for total in sums:
        gate_pre, up_pre, d_hidden = (
            total[:, :block],
            total[:, block : 2 * block],
            total[:, 2 * block :],
        )
        sigmoid_gate = jax.nn.sigmoid(gate_pre)
        activated = gate_pre * sigmoid_gate
        hidden = (activated * up_pre).astype(BF16)
        d_gate = (
            d_hidden * up_pre * sigmoid_gate * (1.0 + gate_pre * (1.0 - sigmoid_gate))
        ).astype(BF16)
        d_up = (d_hidden * activated).astype(BF16)
        acts_own.append(jnp.concatenate([d_gate, d_up, hidden], axis=1))

    halves = {0: acts_own}
    right = list(acts_own)
    left = list(acts_own)
    for step in (1, 2, 3):
        right = [ring(a, 1) for a in right]
        left = [ring(a, -1) for a in left]
        halves[RING - step] = right
        halves[step] = left
    halves[4] = [ring(right[0], 1), ring(left[1], -1)]

    near, far = (0, 7, 1, 6, 2, 5, 3), (4,)
    kept, given = [], []
    for deltas, name in ((near, "out_near"), (far, "out_far")):
        shape = (len(deltas), capacity, 2 * width)
        pieces = [h for delta in deltas for h in halves[delta]]
        keep, give = local_call(
            functools.partial(out_body, deltas),
            name,
            [jax.ShapeDtypeStruct(shape, F32), jax.ShapeDtypeStruct(shape, BF16)],
            [where, w_rows, w_grads] + pieces,
            [pltpu.VMEM((len(pieces) * capacity, units), BF16)],
        )
        kept.append(keep)
        given.append(give)
    swapped = [core_swap(give) for give in lax.optimization_barrier(given)]

    part = width // 2
    pieces = [h for delta in first + rest for h in halves[delta]]
    keep_w, give_w = local_call(
        functools.partial(weight_body, block),
        "weight_grads",
        [jax.ShapeDtypeStruct((part, units), F32), jax.ShapeDtypeStruct((part, units), BF16)],
        [where] + payloads + pieces,
        [pltpu.VMEM((len(pieces) * capacity, units), BF16)],
    )
    swapped, give_w = lax.optimization_barrier((swapped, give_w))
    got_w = lax.ppermute(give_w, "dp", [(0, 1), (1, 0)])
    by_chip = local_call(
        functools.partial(sum_body, near),
        "pair_sum",
        jax.ShapeDtypeStruct((CHIPS, capacity, 2 * width), BF16),
        [where, kept[0], swapped[0], kept[1], swapped[1]],
    )
    arrived = among_chips(by_chip)
    mixed, input_grad = local_call(
        scatter_body,
        "scatter_rows",
        [jax.ShapeDtypeStruct((token_count, width), BF16)] * 2,
        [
            where,
            arrived,
            route_index[None, :],
            route_weight[:, None],
            is_live[:, None].astype(jnp.int32),
        ],
    )
    grads_w = keep_w + got_w.astype(F32)
    return (
        mixed,
        input_grad,
        grads_w[:, :block].T,
        grads_w[:, block : 2 * block].T,
        grads_w[:, 2 * block :].T,
    )


def solution(mesh):
    ways = (("x", "y", "core"), "tensor", "dp")
    chips = Mesh(mesh.devices.reshape(XS, YS, CORES, RING, 2), ways[0] + ways[1:])
    expert, tensor, dp = ways
    tokens = P(expert + (dp,), tensor)
    weight = P(expert, tensor)
    slots = P(expert + (dp,))
    grad = P(expert, (tensor, dp))
    return jax.shard_map(
        on_device,
        mesh=chips,
        in_specs=(tokens, tokens, weight, weight, weight, slots, slots, slots),
        out_specs=(tokens, tokens, grad, grad, grad),
        check_vma=False,
    )
```

```python
import functools

import jax
import jax.numpy as jnp
from jax import lax
from jax.experimental import pallas as pl
from jax.experimental.pallas import tpu as pltpu
from jax.sharding import Mesh
from jax.sharding import PartitionSpec as P

BF16 = jnp.bfloat16
F32 = jnp.float32
XS, YS, CORES, RING = 4, 2, 2, 8
CHIPS = XS * YS
FIRST, LAST = 640, 768
VMEM_LIMIT = 40 * 1024 * 1024
WHOLE = pl.BlockSpec(memory_space=pltpu.VMEM)
SCALARS = pl.BlockSpec(memory_space=pltpu.SMEM)


def dot(left, right, left_dim, right_dim):
    return lax.dot_general(
        left, right, (((left_dim,), (right_dim,)), ((), ())), preferred_element_type=F32
    )


def core_swap(x):
    return lax.ppermute(x, "core", [(0, 1), (1, 0)])


def among_chips(x):
    return lax.all_to_all(x, ("x", "y"), 0, 0, tiled=True)


def ring(x, by):
    return lax.ppermute(x, "tensor", [(z, (z + by) % RING) for z in range(RING)])


def local_call(body, name, out_shape, operands, scratch=()):
    return pl.pallas_call(
        body,
        out_shape=out_shape,
        in_specs=[SCALARS] + [WHOLE] * len(operands[1:]),
        out_specs=jax.tree.map(lambda _: WHOLE, out_shape),
        scratch_shapes=scratch,
        compiler_params=pltpu.CompilerParams(vmem_limit_bytes=VMEM_LIMIT),
        cost_estimate=pl.CostEstimate(flops=1, bytes_accessed=1, transcendentals=0),
        name=name,
    )(*operands)


def pre_body(deltas, where_ref, came_ref, other_ref, w_rows_ref, w_grads_ref, payload_ref, *refs):
    here, core = where_ref[0], where_ref[1]
    size, width = came_ref.shape[1:]
    for n, delta in enumerate(deltas):
        at = lax.rem(here + delta, RING)
        came, other = came_ref[at], other_ref[at]
        payload_ref[n * size : (n + 1) * size, :width] = jnp.where(core == 0, came, other)
        payload_ref[n * size : (n + 1) * size, width:] = jnp.where(core == 0, other, came)
    by_rows = dot(payload_ref[:, :width], w_rows_ref[...], 1, 1)
    by_grads = dot(payload_ref[:, width:], w_grads_ref[...], 1, 1)
    mixed = by_rows[:, FIRST:] + by_grads[:, : LAST - FIRST]
    for n, ref in enumerate(refs):
        rows, kind = slice(n * size, (n + 1) * size), ref.dtype
        ref[:, :FIRST] = by_rows[rows, :FIRST].astype(kind)
        ref[:, FIRST:LAST] = mixed[rows].astype(kind)
        ref[:, LAST:] = by_grads[rows, LAST - FIRST :].astype(kind)


def join(refs, to_ref):
    size = refs[0].shape[0]
    for n, ref in enumerate(refs):
        to_ref[n * size : (n + 1) * size, :] = ref[...]


def out_body(where_ref, w_rows_ref, w_grads_ref, *refs):
    core = where_ref[1]
    keep_ref, give_ref, acts_ref = refs[-3:]
    join(refs[:-3], acts_ref)
    out = dot(acts_ref[:, FIRST:], w_grads_ref[...], 1, 0)
    back = dot(acts_ref[:, :LAST], w_rows_ref[...], 1, 0)
    keep_ref[...] = jnp.where(core == 0, out, back)
    give_ref[...] = jnp.where(core == 0, back, out).astype(BF16)


def weight_body(block, where_ref, *refs):
    dp = where_ref[2]
    payload_refs = refs[:4]
    keep_ref, give_ref, acts_ref, payload_ref = refs[-4:]
    join(refs[4:-4], acts_ref)
    at = 0
    for ref in payload_refs:
        payload_ref[at : at + ref.shape[0], :] = ref[...]
        at += ref.shape[0]
    part = keep_ref.shape[0]
    width = 2 * part

    def product(cols, units):
        return dot(payload_ref[:, cols], acts_ref[:, units], 0, 0)

    by_rows = product(slice(0, width), slice(0, LAST))
    by_grads = product(slice(width, 2 * width), slice(FIRST, acts_ref.shape[1]))
    unit = FIRST + lax.broadcasted_iota(jnp.int32, (part, LAST - FIRST), 1)
    for cols in (slice(0, FIRST), slice(FIRST, LAST), slice(LAST, acts_ref.shape[1])):
        halves = []
        for rows in (slice(0, part), slice(part, width)):
            if cols.stop == FIRST:
                halves.append(by_rows[rows, :FIRST])
            elif cols.start == FIRST:
                halves.append(
                    jnp.where(
                        unit < 2 * block, by_rows[rows, FIRST:], by_grads[rows, : LAST - FIRST]
                    )
                )
            else:
                halves.append(by_grads[rows, LAST - FIRST :])
        keep_ref[:, cols] = jnp.where(dp == 0, halves[0], halves[1])
        give_ref[:, cols] = jnp.where(dp == 0, halves[1], halves[0]).astype(BF16)


def scatter_body(where_ref, came_ref, index_ref, weight_ref, live_ref, mixed_ref, grad_ref):
    total = came_ref[0].astype(F32)
    for n in range(1, CHIPS):
        total = total + came_ref[n].astype(F32)
    token_count, width = mixed_ref.shape
    out_rows = (weight_ref[...] * total[:, :width]).astype(BF16)
    back_rows = jnp.where(live_ref[...] > 0, total[:, width:], 0.0).astype(BF16)
    token = lax.broadcasted_iota(jnp.int32, (token_count, index_ref.shape[1]), 0)
    place = jnp.where(token == index_ref[...], 1.0, 0.0).astype(BF16)
    mixed_ref[...] = dot(place, out_rows, 1, 0).astype(BF16)
    grad_ref[...] = dot(place, back_rows, 1, 0).astype(BF16)


def pair_body(deltas, where_ref, keep_ref, got_ref, keep_last_ref, got_last_ref, out_ref):
    here = where_ref[0]
    size = out_ref.shape[1]
    for n, delta in enumerate(deltas):
        rows = slice(n * size, (n + 1) * size)
        out_ref[lax.rem(here + delta, RING)] = (
            keep_ref[rows] + got_ref[rows].astype(F32)
        ).astype(BF16)
    out_ref[lax.rem(here + RING // 2, RING)] = (
        keep_last_ref[...] + got_last_ref[...].astype(F32)
    ).astype(BF16)


def chip_body(where_ref, a_ref, b_ref, own_ref, give_ref):
    core = where_ref[1]
    totals = []
    for ref in (a_ref, b_ref):
        total = ref[0].astype(F32)
        for n in range(1, CHIPS):
            total = total + ref[n].astype(F32)
        totals.append(total)
    own_ref[...] = jnp.where(core == 0, totals[0], totals[1])
    give_ref[...] = jnp.where(core == 0, totals[1], totals[0]).astype(BF16)


def scatter_body(where_ref, own_ref, got_ref, index_ref, weight_ref, live_ref, mixed_ref, grad_ref):
    core = where_ref[1]
    own, got = own_ref[...], got_ref[...].astype(F32)
    out_rows = (weight_ref[...] * jnp.where(core == 0, own, got)).astype(BF16)
    back_rows = jnp.where(live_ref[...] > 0, jnp.where(core == 0, got, own), 0.0).astype(BF16)
    token = lax.broadcasted_iota(jnp.int32, (mixed_ref.shape[0], index_ref.shape[1]), 0)
    place = jnp.where(token == index_ref[...], 1.0, 0.0).astype(BF16)
    mixed_ref[...] = dot(place, out_rows, 1, 0).astype(BF16)
    grad_ref[...] = dot(place, back_rows, 1, 0).astype(BF16)


def on_device(
    tokens, out_grad, gate_weight, up_weight, down_weight, route_count, route_index, route_gate
):
    capacity = route_index.shape[0]
    token_count, width = tokens.shape
    block = gate_weight.shape[0]
    units = 3 * block
    core = lax.axis_index("core")
    core0 = core == 0
    here = lax.axis_index("tensor")
    where = jnp.stack([here, core, lax.axis_index("dp")]).astype(jnp.int32)
    is_live = jnp.arange(capacity, dtype=jnp.int32) < route_count[0]
    route_weight = jnp.where(is_live, route_gate, 0.0)
    pick = (
        route_index[:, None] == jnp.arange(token_count, dtype=jnp.int32)[None, :]
    ).astype(BF16)
    rows_here = dot(pick, tokens, 1, 0).astype(BF16)
    grads_here = (route_weight[:, None] * dot(pick, out_grad, 1, 0)).astype(BF16)

    w_rows = jnp.concatenate(
        [gate_weight, up_weight, jnp.zeros((LAST - 2 * block, width), BF16)], axis=0
    )
    w_grads = jnp.concatenate(
        [jnp.zeros((2 * block - FIRST, width), BF16), down_weight], axis=0
    )

    mine = jnp.where(core0, rows_here, grads_here)
    got = core_swap(jnp.where(core0, grads_here, rows_here))
    chunks = (jnp.where(core0, mine, got), jnp.where(core0, got, mine))
    pre = {}
    payloads = []
    first, rest = (4, 3, 5), (2, 6, 1, 7, 0)
    for h, piece in enumerate(chunks):
        came = among_chips(jnp.broadcast_to(piece[None], (CHIPS,) + piece.shape))
        other = core_swap(came)
        for deltas, name in ((first, "pre_first"), (rest, "pre_rest")):
            shapes = [jax.ShapeDtypeStruct((len(deltas) * capacity, 2 * width), BF16)]
            for delta in deltas:
                starts = delta == 4 or (delta, h) in ((3, 0), (5, 1))
                shapes.append(jax.ShapeDtypeStruct((capacity, units), BF16 if starts else F32))
            payload, *blocks = local_call(
                functools.partial(pre_body, deltas),
                name,
                shapes,
                [where, came, other, w_rows, w_grads],
            )
            payloads.append(payload)
            pre.update({(delta, h): part for delta, part in zip(deltas, blocks)})

    sums = []
    for h in range(2):
        left_path = (4, 5, 6, 7) if h == 0 else (5, 6, 7)
        right_path = (3, 2, 1) if h == 0 else (4, 3, 2, 1)
        ends = []
        for path, by in ((left_path, -1), (right_path, 1)):
            moving = None
            for delta in path:
                total = pre[delta, h]
                if moving is not None:
                    total = total + moving.astype(F32)
                moving = ring(total.astype(BF16), by)
            ends.append(moving.astype(F32))
        sums.append(pre[0, h] + ends[0] + ends[1])

    acts_own = []
    for total in sums:
        gate_pre, up_pre, d_hidden = (
            total[:, :block],
            total[:, block : 2 * block],
            total[:, 2 * block :],
        )
        sigmoid_gate = jax.nn.sigmoid(gate_pre)
        activated = gate_pre * sigmoid_gate
        hidden = (activated * up_pre).astype(BF16)
        d_gate = (
            d_hidden * up_pre * sigmoid_gate * (1.0 + gate_pre * (1.0 - sigmoid_gate))
        ).astype(BF16)
        d_up = (d_hidden * activated).astype(BF16)
        acts_own.append(jnp.concatenate([d_gate, d_up, hidden], axis=1))

    halves = {0: acts_own}
    right = list(acts_own)
    left = list(acts_own)
    for step in (1, 2, 3):
        right = [ring(a, 1) for a in right]
        left = [ring(a, -1) for a in left]
        halves[RING - step] = right
        halves[step] = left
    halves[4] = [ring(right[0], 1), ring(left[1], -1)]

    near = (0, 7, 1, 6, 2, 5, 3)
    kept, given = [], []
    for h in range(2):
        for deltas, name in ((near, "out_near"), ((4,), "out_far")):
            shape = (len(deltas) * capacity, width)
            keep, give = local_call(
                out_body,
                name,
                [jax.ShapeDtypeStruct(shape, F32), jax.ShapeDtypeStruct(shape, BF16)],
                [where, w_rows, w_grads] + [halves[delta][h] for delta in deltas],
                [pltpu.VMEM((len(deltas) * capacity, units), BF16)],
            )
            kept.append(keep)
            given.append(give)
    arrived = []
    for h in range(2):
        swapped = [core_swap(g) for g in lax.optimization_barrier(given[2 * h : 2 * h + 2])]
        by_chip = local_call(
            functools.partial(pair_body, near),
            "pair_sum",
            jax.ShapeDtypeStruct((CHIPS, capacity, width), BF16),
            [where, kept[2 * h], swapped[0], kept[2 * h + 1], swapped[1]],
        )
        arrived.append(among_chips(by_chip))

    part = width // 2
    pieces = [halves[delta][h] for h in range(2) for delta in first + rest]
    keep_w, give_w = local_call(
        functools.partial(weight_body, block),
        "weight_grads",
        [jax.ShapeDtypeStruct((part, units), F32), jax.ShapeDtypeStruct((part, units), BF16)],
        [where] + payloads + pieces,
        [
            pltpu.VMEM((len(pieces) * capacity, units), BF16),
            pltpu.VMEM((len(pieces) * capacity, 2 * width), BF16),
        ],
    )
    got_w = lax.ppermute(give_w, "dp", [(0, 1), (1, 0)])

    own, give = local_call(
        chip_body,
        "chip_sum",
        [
            jax.ShapeDtypeStruct((capacity, width), F32),
            jax.ShapeDtypeStruct((capacity, width), BF16),
        ],
        [where] + arrived,
    )
    mixed, input_grad = local_call(
        scatter_body,
        "scatter_rows",
        [jax.ShapeDtypeStruct((token_count, width), BF16)] * 2,
        [
            where,
            own,
            core_swap(give),
            route_index[None, :],
            route_weight[:, None],
            is_live[:, None].astype(jnp.int32),
        ],
    )
    grads_w = keep_w + got_w.astype(F32)
    return (
        mixed,
        input_grad,
        grads_w[:, :block].T,
        grads_w[:, block : 2 * block].T,
        grads_w[:, 2 * block :].T,
    )


def solution(mesh):
    ways = (("x", "y", "core"), "tensor", "dp")
    chips = Mesh(mesh.devices.reshape(XS, YS, CORES, RING, 2), ways[0] + ways[1:])
    expert, tensor, dp = ways
    tokens = P(expert + (dp,), tensor)
    weight = P(expert, tensor)
    slots = P(expert + (dp,))
    grad = P(expert, (tensor, dp))
    return jax.shard_map(
        on_device,
        mesh=chips,
        in_specs=(tokens, tokens, weight, weight, weight, slots, slots, slots),
        out_specs=(tokens, tokens, grad, grad, grad),
        check_vma=False,
    )
```

```python
import functools

import jax
import jax.numpy as jnp
from jax import lax
from jax.experimental import pallas as pl
from jax.experimental.pallas import tpu as pltpu
from jax.sharding import Mesh
from jax.sharding import PartitionSpec as P

BF16 = jnp.bfloat16
F32 = jnp.float32
XS, YS, CORES, RING = 4, 2, 2, 8
CHIPS = XS * YS
FIRST, LAST = 640, 768
VMEM_LIMIT = 40 * 1024 * 1024
WHOLE = pl.BlockSpec(memory_space=pltpu.VMEM)
SCALARS = pl.BlockSpec(memory_space=pltpu.SMEM)


def dot(left, right, left_dim, right_dim):
    return lax.dot_general(
        left, right, (((left_dim,), (right_dim,)), ((), ())), preferred_element_type=F32
    )


def core_swap(x):
    return lax.ppermute(x, "core", [(0, 1), (1, 0)])


def among_chips(x):
    return lax.all_to_all(x, ("x", "y"), 0, 0, tiled=True)


def ring(x, by):
    return lax.ppermute(x, "tensor", [(z, (z + by) % RING) for z in range(RING)])


def local_call(body, name, out_shape, operands, scratch=()):
    return pl.pallas_call(
        body,
        out_shape=out_shape,
        in_specs=[SCALARS] + [WHOLE] * len(operands[1:]),
        out_specs=jax.tree.map(lambda _: WHOLE, out_shape),
        scratch_shapes=scratch,
        compiler_params=pltpu.CompilerParams(vmem_limit_bytes=VMEM_LIMIT),
        cost_estimate=pl.CostEstimate(flops=1, bytes_accessed=1, transcendentals=0),
        name=name,
    )(*operands)


def column(row):
    size = row.shape[1]
    same = lax.broadcasted_iota(jnp.int32, (size, size), 0) == lax.broadcasted_iota(
        jnp.int32, (size, size), 1
    )
    return jnp.sum(jnp.where(same, row, 0.0), axis=1, keepdims=True)


def routes(count_ref, index_ref, gate_ref, token_count):
    size = index_ref.shape[1]
    live = lax.broadcasted_iota(jnp.int32, (1, size), 1) < count_ref[0]
    token = lax.broadcasted_iota(jnp.int32, (token_count, size), 0)
    place = jnp.where(token == index_ref[...], 1.0, 0.0).astype(BF16)
    weight = column(jnp.where(live, gate_ref[...], 0.0))
    return place, weight, column(jnp.where(live, 1.0, 0.0))


def gather_body(count_ref, tokens_ref, grads_ref, index_ref, gate_ref, out_ref):
    token_count, width = tokens_ref.shape
    place, weight, _ = routes(count_ref, index_ref, gate_ref, token_count)
    rows = dot(place, tokens_ref[...], 0, 0).astype(BF16)
    grads = (weight * dot(place, grads_ref[...], 0, 0)).astype(BF16)
    for n in range(CHIPS):
        out_ref[n, :, :width] = rows
        out_ref[n, :, width:] = grads


def pre_body(deltas, where_ref, rows_ref, w_rows_ref, w_grads_ref, payload_ref, *refs):
    here = where_ref[0]
    size = rows_ref.shape[1]
    width = rows_ref.shape[2] // 2
    for n, delta in enumerate(deltas):
        payload_ref[n * size : (n + 1) * size, :] = rows_ref[lax.rem(here + delta, RING)]
    by_rows = dot(payload_ref[:, :width], w_rows_ref[...], 1, 1)
    by_grads = dot(payload_ref[:, width:], w_grads_ref[...], 1, 1)
    mixed = by_rows[:, FIRST:] + by_grads[:, : LAST - FIRST]
    for n, ref in enumerate(refs):
        rows, kind = slice(n * size, (n + 1) * size), ref.dtype
        ref[:, :FIRST] = by_rows[rows, :FIRST].astype(kind)
        ref[:, FIRST:LAST] = mixed[rows].astype(kind)
        ref[:, LAST:] = by_grads[rows, LAST - FIRST :].astype(kind)


def join(refs, to_ref):
    size = refs[0].shape[0]
    for n, ref in enumerate(refs):
        to_ref[n * size : (n + 1) * size, :] = ref[...]


def out_body(where_ref, w_rows_ref, w_grads_ref, *refs):
    keep_ref, give_ref, acts_ref = refs[-3:]
    join(refs[:-3], acts_ref)
    size, width = keep_ref.shape[0], w_rows_ref.shape[1]
    out = dot(acts_ref[:, FIRST:], w_grads_ref[...], 1, 0)
    back = dot(acts_ref[:, :LAST], w_rows_ref[...], 1, 0)
    keep_ref[:, :width] = out[:size]
    keep_ref[:, width:] = back[:size]
    give_ref[:, :width] = out[size:].astype(BF16)
    give_ref[:, width:] = back[size:].astype(BF16)


def weight_body(block, where_ref, *refs):
    dp = where_ref[1]
    payload_refs = refs[:4]
    keep_ref, give_ref, acts_ref = refs[-3:]
    join(refs[4:-3], acts_ref)
    part = keep_ref.shape[0]
    width = 2 * part

    def product(cols, units):
        total, at = None, 0
        for ref in payload_refs:
            term = dot(ref[:, cols], acts_ref[at : at + ref.shape[0], units], 0, 0)
            total = term if total is None else total + term
            at += ref.shape[0]
        return total

    by_rows = product(slice(0, width), slice(0, LAST))
    by_grads = product(slice(width, 2 * width), slice(FIRST, acts_ref.shape[1]))
    unit = FIRST + lax.broadcasted_iota(jnp.int32, (part, LAST - FIRST), 1)
    for cols in (slice(0, FIRST), slice(FIRST, LAST), slice(LAST, acts_ref.shape[1])):
        halves = []
        for rows in (slice(0, part), slice(part, width)):
            if cols.stop == FIRST:
                halves.append(by_rows[rows, :FIRST])
            elif cols.start == FIRST:
                halves.append(
                    jnp.where(
                        unit < 2 * block, by_rows[rows, FIRST:], by_grads[rows, : LAST - FIRST]
                    )
                )
            else:
                halves.append(by_grads[rows, LAST - FIRST :])
        keep_ref[:, cols] = jnp.where(dp == 0, halves[0], halves[1])
        give_ref[:, cols] = jnp.where(dp == 0, halves[1], halves[0]).astype(BF16)


def pair_body(deltas, where_ref, keep_ref, got_ref, keep_last_ref, got_last_ref, out_ref):
    here = where_ref[0]
    size = out_ref.shape[1]
    for n, delta in enumerate(deltas):
        rows = slice(n * size, (n + 1) * size)
        out_ref[lax.rem(here + delta, RING)] = (
            keep_ref[rows] + got_ref[rows].astype(F32)
        ).astype(BF16)
    out_ref[lax.rem(here + RING // 2, RING)] = (
        keep_last_ref[...] + got_last_ref[...].astype(F32)
    ).astype(BF16)


def scatter_body(count_ref, came_ref, index_ref, gate_ref, mixed_ref, grad_ref):
    total = came_ref[0].astype(F32)
    for n in range(1, CHIPS):
        total = total + came_ref[n].astype(F32)
    token_count, width = mixed_ref.shape
    place, weight, live = routes(count_ref, index_ref, gate_ref, token_count)
    out_rows = (weight * total[:, :width]).astype(BF16)
    back_rows = jnp.where(live > 0.0, total[:, width:], 0.0).astype(BF16)
    mixed_ref[...] = dot(place, out_rows, 1, 0).astype(BF16)
    grad_ref[...] = dot(place, back_rows, 1, 0).astype(BF16)


def on_device(
    tokens, out_grad, gate_weight, up_weight, down_weight, route_count, route_index, route_gate
):
    capacity = route_index.shape[0]
    token_count, width = tokens.shape
    block = gate_weight.shape[0]
    units = 3 * block
    here = lax.axis_index("tensor")
    where = jnp.stack([here, lax.axis_index("dp")]).astype(jnp.int32)
    routing = [route_index[None, :], route_gate[None, :]]

    w_rows = jnp.concatenate(
        [gate_weight, up_weight, jnp.zeros((LAST - 2 * block, width), BF16)], axis=0
    )
    w_grads = jnp.concatenate(
        [jnp.zeros((2 * block - FIRST, width), BF16), down_weight], axis=0
    )

    copies = local_call(
        gather_body,
        "gather_rows",
        jax.ShapeDtypeStruct((CHIPS, capacity, 2 * width), BF16),
        [route_count, tokens, out_grad] + routing,
    )
    came = among_chips(copies)
    pre = {}
    payloads = []
    first, rest = (4, 3, 5), (2, 6, 1, 7, 0)
    for h, rows in enumerate((came, core_swap(came))):
        for deltas, name in ((first, "pre_first"), (rest, "pre_rest")):
            shapes = [jax.ShapeDtypeStruct((len(deltas) * capacity, 2 * width), BF16)]
            for delta in deltas:
                starts = delta == 4 or (delta, h) in ((3, 0), (5, 1))
                shapes.append(jax.ShapeDtypeStruct((capacity, units), BF16 if starts else F32))
            payload, *blocks = local_call(
                functools.partial(pre_body, deltas), name, shapes, [where, rows, w_rows, w_grads]
            )
            payloads.append(payload)
            pre.update({(delta, h): part for delta, part in zip(deltas, blocks)})

    own_left, own_right = ring(pre[4, 0], -1), ring(pre[3, 0], 1)
    own_left, own_right, payloads[2] = lax.optimization_barrier(
        (own_left, own_right, payloads[2])
    )
    sums = []
    for h, ways in (
        (0, ((own_left, (5, 6, 7), -1), (own_right, (2, 1), 1))),
        (1, ((None, (5, 6, 7), -1), (None, (4, 3, 2, 1), 1))),
    ):
        total = pre[0, h]
        for moving, path, by in ways:
            for delta in path:
                block_sum = pre[delta, h]
                if moving is not None:
                    block_sum = block_sum + moving.astype(F32)
                moving = ring(block_sum.astype(BF16), by)
            total = total + moving.astype(F32)
        sums.append(total)

    acts_own = []
    for total in sums:
        gate_pre, up_pre, d_hidden = (
            total[:, :block],
            total[:, block : 2 * block],
            total[:, 2 * block :],
        )
        sigmoid_gate = jax.nn.sigmoid(gate_pre)
        activated = gate_pre * sigmoid_gate
        hidden = (activated * up_pre).astype(BF16)
        d_gate = (
            d_hidden * up_pre * sigmoid_gate * (1.0 + gate_pre * (1.0 - sigmoid_gate))
        ).astype(BF16)
        d_up = (d_hidden * activated).astype(BF16)
        acts_own.append(jnp.concatenate([d_gate, d_up, hidden], axis=1))

    halves = {0: acts_own}
    right = list(acts_own)
    left = list(acts_own)
    for step in (1, 2, 3):
        right = [ring(a, 1) for a in right]
        left = [ring(a, -1) for a in left]
        halves[RING - step] = right
        halves[step] = left
    halves[4] = [ring(right[0], 1), ring(left[1], -1)]

    near, far = (0, 7, 1, 6, 2, 5, 3), (4,)
    kept, given = [], []
    for deltas, name in ((near, "out_near"), (far, "out_far")):
        shape = (len(deltas) * capacity, 2 * width)
        keep, give = local_call(
            out_body,
            name,
            [jax.ShapeDtypeStruct(shape, F32), jax.ShapeDtypeStruct(shape, BF16)],
            [where, w_rows, w_grads] + [halves[delta][h] for h in range(2) for delta in deltas],
            [pltpu.VMEM((2 * len(deltas) * capacity, units), BF16)],
        )
        kept.append(keep)
        given.append(give)
    swapped = [core_swap(give) for give in lax.optimization_barrier(given)]

    part = width // 2
    pieces = [halves[delta][h] for h in range(2) for delta in first + rest]
    keep_w, give_w = local_call(
        functools.partial(weight_body, block),
        "weight_grads",
        [jax.ShapeDtypeStruct((part, units), F32), jax.ShapeDtypeStruct((part, units), BF16)],
        [where] + payloads + pieces,
        [pltpu.VMEM((len(pieces) * capacity, units), BF16)],
    )
    swapped, give_w = lax.optimization_barrier((swapped, give_w))
    got_w = lax.ppermute(give_w, "dp", [(0, 1), (1, 0)])
    by_chip = local_call(
        functools.partial(pair_body, near),
        "pair_sum",
        jax.ShapeDtypeStruct((CHIPS, capacity, 2 * width), BF16),
        [where, kept[0], swapped[0], kept[1], swapped[1]],
    )
    arrived = among_chips(by_chip)
    mixed, input_grad = local_call(
        scatter_body,
        "scatter_rows",
        [jax.ShapeDtypeStruct((token_count, width), BF16)] * 2,
        [route_count, arrived] + routing,
    )
    grads_w = keep_w + got_w.astype(F32)
    return (
        mixed,
        input_grad,
        grads_w[:, :block].T,
        grads_w[:, block : 2 * block].T,
        grads_w[:, 2 * block :].T,
    )


def solution(mesh):
    ways = (("x", "y", "core"), "tensor", "dp")
    chips = Mesh(mesh.devices.reshape(XS, YS, CORES, RING, 2), ways[0] + ways[1:])
    expert, tensor, dp = ways
    tokens = P(expert + (dp,), tensor)
    weight = P(expert, tensor)
    slots = P(expert + (dp,))
    grad = P(expert, (tensor, dp))
    return jax.shard_map(
        on_device,
        mesh=chips,
        in_specs=(tokens, tokens, weight, weight, weight, slots, slots, slots),
        out_specs=(tokens, tokens, grad, grad, grad),
        check_vma=False,
    )
```

```python
import functools

import jax
import jax.numpy as jnp
from jax import lax
from jax.experimental import pallas as pl
from jax.experimental.pallas import tpu as pltpu
from jax.sharding import Mesh
from jax.sharding import PartitionSpec as P

BF16 = jnp.bfloat16
F32 = jnp.float32
XS, YS, CORES, RING = 4, 2, 2, 8
CHIPS = XS * YS
FIRST, LAST = 640, 768
VMEM_LIMIT = 40 * 1024 * 1024
FETCH_LIMIT = 60 * 1024 * 1024
WHOLE = pl.BlockSpec(memory_space=pltpu.VMEM)
SCALARS = pl.BlockSpec(memory_space=pltpu.SMEM)


def dot(left, right, left_dim, right_dim):
    return lax.dot_general(
        left, right, (((left_dim,), (right_dim,)), ((), ())), preferred_element_type=F32
    )


def core_swap(x):
    return lax.ppermute(x, "core", [(0, 1), (1, 0)])


def among_chips(x):
    return lax.all_to_all(x, ("x", "y"), 0, 0, tiled=True)


def along_y(x):
    return lax.ppermute(x, "y", [(0, 1), (1, 0)])


def along_x(x, by):
    return lax.ppermute(x, "x", [(i, (i + by) % XS) for i in range(XS)])


def ring(x, by):
    return lax.ppermute(x, "tensor", [(z, (z + by) % RING) for z in range(RING)])


def fetched(x):
    return pl.BlockSpec(x.shape, lambda i: (0,) * x.ndim)


def local_call(body, name, out_shape, operands, scratch=(), fetch=False):
    return pl.pallas_call(
        body,
        out_shape=out_shape,
        grid=(1,) if fetch else (),
        in_specs=[SCALARS] + [fetched(x) if fetch else WHOLE for x in operands[1:]],
        out_specs=jax.tree.map(lambda _: WHOLE, out_shape),
        scratch_shapes=scratch,
        compiler_params=pltpu.CompilerParams(
            vmem_limit_bytes=FETCH_LIMIT if fetch else VMEM_LIMIT
        ),
        cost_estimate=pl.CostEstimate(flops=1, bytes_accessed=1, transcendentals=0),
        name=name,
    )(*operands)


def column(row):
    size = row.shape[1]
    same = lax.broadcasted_iota(jnp.int32, (size, size), 0) == lax.broadcasted_iota(
        jnp.int32, (size, size), 1
    )
    return jnp.sum(jnp.where(same, row, 0.0), axis=1, keepdims=True)


def routes(count_ref, index_ref, gate_ref, token_count):
    size = index_ref.shape[1]
    live = lax.broadcasted_iota(jnp.int32, (1, size), 1) < count_ref[0]
    token = lax.broadcasted_iota(jnp.int32, (token_count, size), 0)
    place = jnp.where(token == index_ref[...], 1.0, 0.0).astype(BF16)
    weight = column(jnp.where(live, gate_ref[...], 0.0))
    return place, weight, column(jnp.where(live, 1.0, 0.0))


def gather_body(count_ref, tokens_ref, grads_ref, index_ref, gate_ref, out_ref):
    token_count, width = tokens_ref.shape
    place, weight, _ = routes(count_ref, index_ref, gate_ref, token_count)
    rows = dot(place, tokens_ref[...], 0, 0).astype(BF16)
    grads = (weight * dot(place, grads_ref[...], 0, 0)).astype(BF16)
    out_ref[:, :width] = rows
    out_ref[:, width:] = grads


def relative(where_ref, delta):
    chip = lax.rem(where_ref[0] + delta, RING)
    x = lax.rem(lax.div(chip, YS) - where_ref[2] + XS, XS)
    y = lax.rem(lax.rem(chip, YS) + where_ref[3], YS)
    return x, y


def pre_body(deltas, where_ref, rows_ref, w_rows_ref, w_grads_ref, payload_ref, *refs):
    size = rows_ref.shape[1]
    width = rows_ref.shape[2] // 2
    for n, delta in enumerate(deltas):
        x, y = relative(where_ref, delta)
        payload_ref[n * size : (n + 1) * size, :] = rows_ref[x * YS + y]
    by_rows = dot(payload_ref[:, :width], w_rows_ref[...], 1, 1)
    by_grads = dot(payload_ref[:, width:], w_grads_ref[...], 1, 1)
    mixed = by_rows[:, FIRST:] + by_grads[:, : LAST - FIRST]
    for n, ref in enumerate(refs):
        rows, kind = slice(n * size, (n + 1) * size), ref.dtype
        ref[:, :FIRST] = by_rows[rows, :FIRST].astype(kind)
        ref[:, FIRST:LAST] = mixed[rows].astype(kind)
        ref[:, LAST:] = by_grads[rows, LAST - FIRST :].astype(kind)


def join(refs, to_ref):
    size = refs[0].shape[0]
    for n, ref in enumerate(refs):
        to_ref[n * size : (n + 1) * size, :] = ref[...]


def out_body(where_ref, w_rows_ref, w_grads_ref, *refs):
    keep_ref, give_ref, acts_ref = refs[-3:]
    join(refs[:-3], acts_ref)
    size, width = keep_ref.shape[0], w_rows_ref.shape[1]
    out = dot(acts_ref[:, FIRST:], w_grads_ref[...], 1, 0)
    back = dot(acts_ref[:, :LAST], w_rows_ref[...], 1, 0)
    keep_ref[:, :width] = out[:size]
    keep_ref[:, width:] = back[:size]
    give_ref[:, :width] = out[size:].astype(BF16)
    give_ref[:, width:] = back[size:].astype(BF16)


def weight_body(block, where_ref, *refs):
    dp = where_ref[1]
    payload_refs = refs[:4]
    keep_ref, give_ref, acts_ref = refs[-3:]
    join(refs[4:-3], acts_ref)
    part = keep_ref.shape[0]
    width = 2 * part

    def product(cols, units):
        total, at = None, 0
        for ref in payload_refs:
            term = dot(ref[:, cols], acts_ref[at : at + ref.shape[0], units], 0, 0)
            total = term if total is None else total + term
            at += ref.shape[0]
        return total

    by_rows = product(slice(0, width), slice(0, LAST))
    by_grads = product(slice(width, 2 * width), slice(FIRST, acts_ref.shape[1]))
    unit = FIRST + lax.broadcasted_iota(jnp.int32, (part, LAST - FIRST), 1)
    for cols in (slice(0, FIRST), slice(FIRST, LAST), slice(LAST, acts_ref.shape[1])):
        halves = []
        for rows in (slice(0, part), slice(part, width)):
            if cols.stop == FIRST:
                halves.append(by_rows[rows, :FIRST])
            elif cols.start == FIRST:
                halves.append(
                    jnp.where(
                        unit < 2 * block, by_rows[rows, FIRST:], by_grads[rows, : LAST - FIRST]
                    )
                )
            else:
                halves.append(by_grads[rows, LAST - FIRST :])
        keep_ref[:, cols] = jnp.where(dp == 0, halves[0], halves[1])
        give_ref[:, cols] = jnp.where(dp == 0, halves[1], halves[0]).astype(BF16)


def pair_body(deltas, where_ref, keep_ref, got_ref, keep_last_ref, got_last_ref, out_ref):
    here, x = where_ref[0], where_ref[2]
    size = out_ref.shape[2]

    def place(delta):
        chip = lax.rem(here + delta, RING)
        return lax.rem(lax.div(chip, YS) - x + XS, XS), lax.rem(chip, YS)

    for n, delta in enumerate(deltas):
        rows = slice(n * size, (n + 1) * size)
        out_ref[place(delta)] = (
            keep_ref[rows] + got_ref[rows].astype(F32)
        ).astype(BF16)
    out_ref[place(RING // 2)] = (
        keep_last_ref[...] + got_last_ref[...].astype(F32)
    ).astype(BF16)


def column_body(y_ref, *refs):
    y = y_ref[0]
    stay_ref, leave_ref = refs[-2:]
    stay = sum(ref[y].astype(F32) for ref in refs[:-2])
    leave = sum(ref[1 - y].astype(F32) for ref in refs[:-2])
    stay_ref[...] = stay
    leave_ref[...] = leave.astype(BF16)


def scatter_body(count_ref, stay_ref, got_ref, index_ref, gate_ref, mixed_ref, grad_ref):
    total = stay_ref[...] + got_ref[...].astype(F32)
    token_count, width = mixed_ref.shape
    place, weight, live = routes(count_ref, index_ref, gate_ref, token_count)
    out_rows = (weight * total[:, :width]).astype(BF16)
    back_rows = jnp.where(live > 0.0, total[:, width:], 0.0).astype(BF16)
    mixed_ref[...] = dot(place, out_rows, 1, 0).astype(BF16)
    grad_ref[...] = dot(place, back_rows, 1, 0).astype(BF16)


def on_device(
    tokens, out_grad, gate_weight, up_weight, down_weight, route_count, route_index, route_gate
):
    capacity = route_index.shape[0]
    token_count, width = tokens.shape
    block = gate_weight.shape[0]
    units = 3 * block
    here = lax.axis_index("tensor")
    where = jnp.stack([here, lax.axis_index("dp"), lax.axis_index("x"), lax.axis_index("y")]).astype(jnp.int32)
    routing = [route_index[None, :], route_gate[None, :]]

    w_rows = jnp.concatenate(
        [gate_weight, up_weight, jnp.zeros((LAST - 2 * block, width), BF16)], axis=0
    )
    w_grads = jnp.concatenate(
        [jnp.zeros((2 * block - FIRST, width), BF16), down_weight], axis=0
    )

    piece = local_call(
        gather_body,
        "gather_rows",
        jax.ShapeDtypeStruct((capacity, 2 * width), BF16),
        [route_count, tokens, out_grad] + routing,
        fetch=True,
    )
    near_y = [piece] + [along_x(piece, XS - by) for by in (1, 2, 3)]
    far_y = [along_y(block_rows) for block_rows in near_y]
    came = jnp.stack([block_rows for pair in zip(near_y, far_y) for block_rows in pair])
    rows = [came, core_swap(came)]
    pre = {}
    payloads = []
    first, rest = (4, 3, 5), (2, 6, 1, 7, 0)
    for deltas, name in ((first, "pre_first"), (rest, "pre_rest")):
        for h in range(2):
            shapes = [jax.ShapeDtypeStruct((len(deltas) * capacity, 2 * width), BF16)]
            for delta in deltas:
                starts = delta == 4 or (delta, h) in ((3, 0), (5, 1))
                shapes.append(jax.ShapeDtypeStruct((capacity, units), BF16 if starts else F32))
            payload, *blocks = local_call(
                functools.partial(pre_body, deltas),
                name,
                shapes,
                [where, rows[h], w_rows, w_grads],
            )
            payloads.append(payload)
            pre.update({(delta, h): part for delta, part in zip(deltas, blocks)})
        if deltas is first:
            rows[0], payloads[1] = lax.optimization_barrier((rows[0], payloads[1]))

    own_left, own_right = ring(pre[4, 0], -1), ring(pre[3, 0], 1)
    own_left, own_right, payloads[1] = lax.optimization_barrier(
        (own_left, own_right, payloads[1])
    )
    sums = []
    for h, ways in (
        (0, ((own_left, (5, 6, 7), -1), (own_right, (2, 1), 1))),
        (1, ((None, (5, 6, 7), -1), (None, (4, 3, 2, 1), 1))),
    ):
        total = pre[0, h]
        for moving, path, by in ways:
            for delta in path:
                block_sum = pre[delta, h]
                if moving is not None:
                    block_sum = block_sum + moving.astype(F32)
                moving = ring(block_sum.astype(BF16), by)
            total = total + moving.astype(F32)
        sums.append(total)

    acts_own = []
    for total in sums:
        gate_pre, up_pre, d_hidden = (
            total[:, :block],
            total[:, block : 2 * block],
            total[:, 2 * block :],
        )
        sigmoid_gate = jax.nn.sigmoid(gate_pre)
        activated = gate_pre * sigmoid_gate
        hidden = (activated * up_pre).astype(BF16)
        d_gate = (
            d_hidden * up_pre * sigmoid_gate * (1.0 + gate_pre * (1.0 - sigmoid_gate))
        ).astype(BF16)
        d_up = (d_hidden * activated).astype(BF16)
        acts_own.append(jnp.concatenate([d_gate, d_up, hidden], axis=1))

    halves = {0: acts_own}
    right = list(acts_own)
    left = list(acts_own)
    for step in (1, 2, 3):
        right = [ring(a, 1) for a in right]
        left = [ring(a, -1) for a in left]
        halves[RING - step] = right
        halves[step] = left
    halves[4] = [ring(right[0], 1), ring(left[1], -1)]

    near, far = (0, 7, 1, 6, 2, 5, 3), (4,)
    kept, given = [], []
    for deltas, name in ((near, "out_near"), (far, "out_far")):
        shape = (len(deltas) * capacity, 2 * width)
        keep, give = local_call(
            out_body,
            name,
            [jax.ShapeDtypeStruct(shape, F32), jax.ShapeDtypeStruct(shape, BF16)],
            [where, w_rows, w_grads] + [halves[delta][h] for h in range(2) for delta in deltas],
            [pltpu.VMEM((2 * len(deltas) * capacity, units), BF16)],
        )
        kept.append(keep)
        given.append(give)
    swapped = [core_swap(give) for give in lax.optimization_barrier(given)]

    part = width // 2
    pieces = [halves[delta][h] for deltas in (first, rest) for h in range(2) for delta in deltas]
    keep_w, give_w = local_call(
        functools.partial(weight_body, block),
        "weight_grads",
        [jax.ShapeDtypeStruct((part, units), F32), jax.ShapeDtypeStruct((part, units), BF16)],
        [where] + payloads + pieces,
        [pltpu.VMEM((len(pieces) * capacity, units), BF16)],
    )
    swapped, give_w = lax.optimization_barrier((swapped, give_w))
    got_w = lax.ppermute(give_w, "dp", [(0, 1), (1, 0)])
    by_chip = local_call(
        functools.partial(pair_body, near),
        "pair_sum",
        jax.ShapeDtypeStruct((XS, YS, capacity, 2 * width), BF16),
        [where, kept[0], swapped[0], kept[1], swapped[1]],
    )
    along = [by_chip[0]] + [along_x(by_chip[by], by) for by in (1, 3, 2)]
    stay, leave = local_call(
        column_body,
        "x_sum",
        [
            jax.ShapeDtypeStruct((capacity, 2 * width), F32),
            jax.ShapeDtypeStruct((capacity, 2 * width), BF16),
        ],
        [lax.axis_index("y")[None].astype(jnp.int32)] + along,
    )
    arrived = (stay, lax.ppermute(leave, "y", [(0, 1), (1, 0)]))
    mixed, input_grad = local_call(
        scatter_body,
        "scatter_rows",
        [jax.ShapeDtypeStruct((token_count, width), BF16)] * 2,
        [route_count, *arrived] + routing,
    )
    grads_w = keep_w + got_w.astype(F32)
    return (
        mixed,
        input_grad,
        grads_w[:, :block].T,
        grads_w[:, block : 2 * block].T,
        grads_w[:, 2 * block :].T,
    )


def solution(mesh):
    ways = (("x", "y", "core"), "tensor", "dp")
    chips = Mesh(mesh.devices.reshape(XS, YS, CORES, RING, 2), ways[0] + ways[1:])
    expert, tensor, dp = ways
    tokens = P(expert + (dp,), tensor)
    weight = P(expert, tensor)
    slots = P(expert + (dp,))
    grad = P(expert, (tensor, dp))
    return jax.shard_map(
        on_device,
        mesh=chips,
        in_specs=(tokens, tokens, weight, weight, weight, slots, slots, slots),
        out_specs=(tokens, tokens, grad, grad, grad),
        check_vma=False,
    )
```

```python
import functools

import jax
import jax.numpy as jnp
from jax import lax
from jax.experimental import pallas as pl
from jax.experimental.pallas import tpu as pltpu
from jax.sharding import Mesh
from jax.sharding import PartitionSpec as P

BF16 = jnp.bfloat16
F32 = jnp.float32
XS, YS, CORES, RING = 4, 2, 2, 8
CHIPS = XS * YS
FIRST, LAST = 640, 768
VMEM_LIMIT = 40 * 1024 * 1024
FETCH_LIMIT = 60 * 1024 * 1024
WHOLE = pl.BlockSpec(memory_space=pltpu.VMEM)
SCALARS = pl.BlockSpec(memory_space=pltpu.SMEM)


def dot(left, right, left_dim, right_dim):
    return lax.dot_general(
        left, right, (((left_dim,), (right_dim,)), ((), ())), preferred_element_type=F32
    )


def core_swap(x):
    return lax.ppermute(x, "core", [(0, 1), (1, 0)])


def among_chips(x):
    return lax.all_to_all(x, ("x", "y"), 0, 0, tiled=True)


def along_x(x, by):
    return lax.ppermute(x, "x", [(i, (i + by) % XS) for i in range(XS)])


def ring(x, by):
    return lax.ppermute(x, "tensor", [(z, (z + by) % RING) for z in range(RING)])


def fetched(x):
    return pl.BlockSpec(x.shape, lambda i: (0,) * x.ndim)


def local_call(body, name, out_shape, operands, scratch=(), fetch=False):
    return pl.pallas_call(
        body,
        out_shape=out_shape,
        grid=(1,) if fetch else (),
        in_specs=[SCALARS] + [fetched(x) if fetch else WHOLE for x in operands[1:]],
        out_specs=jax.tree.map(lambda _: WHOLE, out_shape),
        scratch_shapes=scratch,
        compiler_params=pltpu.CompilerParams(
            vmem_limit_bytes=FETCH_LIMIT if fetch else VMEM_LIMIT
        ),
        cost_estimate=pl.CostEstimate(flops=1, bytes_accessed=1, transcendentals=0),
        name=name,
    )(*operands)


def column(row):
    size = row.shape[1]
    same = lax.broadcasted_iota(jnp.int32, (size, size), 0) == lax.broadcasted_iota(
        jnp.int32, (size, size), 1
    )
    return jnp.sum(jnp.where(same, row, 0.0), axis=1, keepdims=True)


def routes(count_ref, index_ref, gate_ref, token_count):
    size = index_ref.shape[1]
    live = lax.broadcasted_iota(jnp.int32, (1, size), 1) < count_ref[0]
    token = lax.broadcasted_iota(jnp.int32, (token_count, size), 0)
    place = jnp.where(token == index_ref[...], 1.0, 0.0).astype(BF16)
    weight = column(jnp.where(live, gate_ref[...], 0.0))
    return place, weight, column(jnp.where(live, 1.0, 0.0))


def gather_body(count_ref, tokens_ref, grads_ref, index_ref, gate_ref, out_ref):
    token_count, width = tokens_ref.shape
    place, weight, _ = routes(count_ref, index_ref, gate_ref, token_count)
    rows = dot(place, tokens_ref[...], 0, 0).astype(BF16)
    grads = (weight * dot(place, grads_ref[...], 0, 0)).astype(BF16)
    for n in range(CHIPS):
        out_ref[n, :, :width] = rows
        out_ref[n, :, width:] = grads


def pre_body(deltas, where_ref, rows_ref, w_rows_ref, w_grads_ref, payload_ref, *refs):
    here = where_ref[0]
    size = rows_ref.shape[1]
    width = rows_ref.shape[2] // 2
    for n, delta in enumerate(deltas):
        payload_ref[n * size : (n + 1) * size, :] = rows_ref[lax.rem(here + delta, RING)]
    by_rows = dot(payload_ref[:, :width], w_rows_ref[...], 1, 1)
    by_grads = dot(payload_ref[:, width:], w_grads_ref[...], 1, 1)
    mixed = by_rows[:, FIRST:] + by_grads[:, : LAST - FIRST]
    for n, ref in enumerate(refs):
        rows, kind = slice(n * size, (n + 1) * size), ref.dtype
        ref[:, :FIRST] = by_rows[rows, :FIRST].astype(kind)
        ref[:, FIRST:LAST] = mixed[rows].astype(kind)
        ref[:, LAST:] = by_grads[rows, LAST - FIRST :].astype(kind)


def join(refs, to_ref):
    size = refs[0].shape[0]
    for n, ref in enumerate(refs):
        to_ref[n * size : (n + 1) * size, :] = ref[...]


def out_body(where_ref, w_rows_ref, w_grads_ref, *refs):
    keep_ref, give_ref, acts_ref = refs[-3:]
    join(refs[:-3], acts_ref)
    size, width = keep_ref.shape[0], w_rows_ref.shape[1]
    out = dot(acts_ref[:, FIRST:], w_grads_ref[...], 1, 0)
    back = dot(acts_ref[:, :LAST], w_rows_ref[...], 1, 0)
    keep_ref[:, :width] = out[:size]
    keep_ref[:, width:] = back[:size]
    give_ref[:, :width] = out[size:].astype(BF16)
    give_ref[:, width:] = back[size:].astype(BF16)


def weight_body(block, where_ref, *refs):
    dp = where_ref[1]
    payload_refs = refs[:4]
    keep_ref, give_ref, acts_ref = refs[-3:]
    join(refs[4:-3], acts_ref)
    part = keep_ref.shape[0]
    width = 2 * part

    def product(cols, units):
        total, at = None, 0
        for ref in payload_refs:
            term = dot(ref[:, cols], acts_ref[at : at + ref.shape[0], units], 0, 0)
            total = term if total is None else total + term
            at += ref.shape[0]
        return total

    by_rows = product(slice(0, width), slice(0, LAST))
    by_grads = product(slice(width, 2 * width), slice(FIRST, acts_ref.shape[1]))
    unit = FIRST + lax.broadcasted_iota(jnp.int32, (part, LAST - FIRST), 1)
    for cols in (slice(0, FIRST), slice(FIRST, LAST), slice(LAST, acts_ref.shape[1])):
        halves = []
        for rows in (slice(0, part), slice(part, width)):
            if cols.stop == FIRST:
                halves.append(by_rows[rows, :FIRST])
            elif cols.start == FIRST:
                halves.append(
                    jnp.where(
                        unit < 2 * block, by_rows[rows, FIRST:], by_grads[rows, : LAST - FIRST]
                    )
                )
            else:
                halves.append(by_grads[rows, LAST - FIRST :])
        keep_ref[:, cols] = jnp.where(dp == 0, halves[0], halves[1])
        give_ref[:, cols] = jnp.where(dp == 0, halves[1], halves[0]).astype(BF16)


def pair_body(deltas, where_ref, keep_ref, got_ref, keep_last_ref, got_last_ref, out_ref):
    here, x = where_ref[0], where_ref[2]
    size = out_ref.shape[2]

    def place(delta):
        chip = lax.rem(here + delta, RING)
        return lax.rem(lax.div(chip, YS) - x + XS, XS), lax.rem(chip, YS)

    for n, delta in enumerate(deltas):
        rows = slice(n * size, (n + 1) * size)
        out_ref[place(delta)] = (
            keep_ref[rows] + got_ref[rows].astype(F32)
        ).astype(BF16)
    out_ref[place(RING // 2)] = (
        keep_last_ref[...] + got_last_ref[...].astype(F32)
    ).astype(BF16)


def column_body(y_ref, *refs):
    y = y_ref[0]
    stay_ref, leave_ref = refs[-2:]
    stay = sum(ref[y].astype(F32) for ref in refs[:-2])
    leave = sum(ref[1 - y].astype(F32) for ref in refs[:-2])
    stay_ref[...] = stay
    leave_ref[...] = leave.astype(BF16)


def scatter_body(count_ref, stay_ref, got_ref, index_ref, gate_ref, mixed_ref, grad_ref):
    total = stay_ref[...] + got_ref[...].astype(F32)
    token_count, width = mixed_ref.shape
    place, weight, live = routes(count_ref, index_ref, gate_ref, token_count)
    out_rows = (weight * total[:, :width]).astype(BF16)
    back_rows = jnp.where(live > 0.0, total[:, width:], 0.0).astype(BF16)
    mixed_ref[...] = dot(place, out_rows, 1, 0).astype(BF16)
    grad_ref[...] = dot(place, back_rows, 1, 0).astype(BF16)


def on_device(
    tokens, out_grad, gate_weight, up_weight, down_weight, route_count, route_index, route_gate
):
    capacity = route_index.shape[0]
    token_count, width = tokens.shape
    block = gate_weight.shape[0]
    units = 3 * block
    here = lax.axis_index("tensor")
    where = jnp.stack([here, lax.axis_index("dp"), lax.axis_index("x")]).astype(jnp.int32)
    routing = [route_index[None, :], route_gate[None, :]]

    w_rows = jnp.concatenate(
        [gate_weight, up_weight, jnp.zeros((LAST - 2 * block, width), BF16)], axis=0
    )
    w_grads = jnp.concatenate(
        [jnp.zeros((2 * block - FIRST, width), BF16), down_weight], axis=0
    )

    copies = local_call(
        gather_body,
        "gather_rows",
        jax.ShapeDtypeStruct((CHIPS, capacity, 2 * width), BF16),
        [route_count, tokens, out_grad] + routing,
        fetch=True,
    )
    came = among_chips(copies)
    rows = [came, core_swap(came)]
    pre = {}
    payloads = []
    first, rest = (4, 3, 5), (2, 6, 1, 7, 0)
    for deltas, name in ((first, "pre_first"), (rest, "pre_rest")):
        for h in range(2):
            shapes = [jax.ShapeDtypeStruct((len(deltas) * capacity, 2 * width), BF16)]
            for delta in deltas:
                starts = delta == 4 or (delta, h) in ((3, 0), (5, 1))
                shapes.append(jax.ShapeDtypeStruct((capacity, units), BF16 if starts else F32))
            payload, *blocks = local_call(
                functools.partial(pre_body, deltas),
                name,
                shapes,
                [where, rows[h], w_rows, w_grads],
            )
            payloads.append(payload)
            pre.update({(delta, h): part for delta, part in zip(deltas, blocks)})
        if deltas is first:
            rows[0], payloads[1] = lax.optimization_barrier((rows[0], payloads[1]))

    own_left, own_right = ring(pre[4, 0], -1), ring(pre[3, 0], 1)
    own_left, own_right, payloads[1] = lax.optimization_barrier(
        (own_left, own_right, payloads[1])
    )
    sums = []
    for h, ways in (
        (0, ((own_left, (5, 6, 7), -1), (own_right, (2, 1), 1))),
        (1, ((None, (5, 6, 7), -1), (None, (4, 3, 2, 1), 1))),
    ):
        total = pre[0, h]
        for moving, path, by in ways:
            for delta in path:
                block_sum = pre[delta, h]
                if moving is not None:
                    block_sum = block_sum + moving.astype(F32)
                moving = ring(block_sum.astype(BF16), by)
            total = total + moving.astype(F32)
        sums.append(total)

    acts_own = []
    for total in sums:
        gate_pre, up_pre, d_hidden = (
            total[:, :block],
            total[:, block : 2 * block],
            total[:, 2 * block :],
        )
        sigmoid_gate = jax.nn.sigmoid(gate_pre)
        activated = gate_pre * sigmoid_gate
        hidden = (activated * up_pre).astype(BF16)
        d_gate = (
            d_hidden * up_pre * sigmoid_gate * (1.0 + gate_pre * (1.0 - sigmoid_gate))
        ).astype(BF16)
        d_up = (d_hidden * activated).astype(BF16)
        acts_own.append(jnp.concatenate([d_gate, d_up, hidden], axis=1))

    halves = {0: acts_own}
    right = list(acts_own)
    left = list(acts_own)
    for step in (1, 2, 3):
        right = [ring(a, 1) for a in right]
        left = [ring(a, -1) for a in left]
        halves[RING - step] = right
        halves[step] = left
    halves[4] = [ring(right[0], 1), ring(left[1], -1)]

    near, far = (0, 7, 1, 6, 2, 5, 3), (4,)
    kept, given = [], []
    for deltas, name in ((near, "out_near"), (far, "out_far")):
        shape = (len(deltas) * capacity, 2 * width)
        keep, give = local_call(
            out_body,
            name,
            [jax.ShapeDtypeStruct(shape, F32), jax.ShapeDtypeStruct(shape, BF16)],
            [where, w_rows, w_grads] + [halves[delta][h] for h in range(2) for delta in deltas],
            [pltpu.VMEM((2 * len(deltas) * capacity, units), BF16)],
        )
        kept.append(keep)
        given.append(give)
    swapped = [core_swap(give) for give in lax.optimization_barrier(given)]

    part = width // 2
    pieces = [halves[delta][h] for deltas in (first, rest) for h in range(2) for delta in deltas]
    keep_w, give_w = local_call(
        functools.partial(weight_body, block),
        "weight_grads",
        [jax.ShapeDtypeStruct((part, units), F32), jax.ShapeDtypeStruct((part, units), BF16)],
        [where] + payloads + pieces,
        [pltpu.VMEM((len(pieces) * capacity, units), BF16)],
    )
    swapped, give_w = lax.optimization_barrier((swapped, give_w))
    got_w = lax.ppermute(give_w, "dp", [(0, 1), (1, 0)])
    by_chip = local_call(
        functools.partial(pair_body, near),
        "pair_sum",
        jax.ShapeDtypeStruct((XS, YS, capacity, 2 * width), BF16),
        [where, kept[0], swapped[0], kept[1], swapped[1]],
    )
    along = [by_chip[0]] + [along_x(by_chip[by], by) for by in (1, 3, 2)]
    stay, leave = local_call(
        column_body,
        "x_sum",
        [
            jax.ShapeDtypeStruct((capacity, 2 * width), F32),
            jax.ShapeDtypeStruct((capacity, 2 * width), BF16),
        ],
        [lax.axis_index("y")[None].astype(jnp.int32)] + along,
    )
    arrived = (stay, lax.ppermute(leave, "y", [(0, 1), (1, 0)]))
    mixed, input_grad = local_call(
        scatter_body,
        "scatter_rows",
        [jax.ShapeDtypeStruct((token_count, width), BF16)] * 2,
        [route_count, *arrived] + routing,
    )
    grads_w = keep_w + got_w.astype(F32)
    return (
        mixed,
        input_grad,
        grads_w[:, :block].T,
        grads_w[:, block : 2 * block].T,
        grads_w[:, 2 * block :].T,
    )


def solution(mesh):
    ways = (("x", "y", "core"), "tensor", "dp")
    chips = Mesh(mesh.devices.reshape(XS, YS, CORES, RING, 2), ways[0] + ways[1:])
    expert, tensor, dp = ways
    tokens = P(expert + (dp,), tensor)
    weight = P(expert, tensor)
    slots = P(expert + (dp,))
    grad = P(expert, (tensor, dp))
    return jax.shard_map(
        on_device,
        mesh=chips,
        in_specs=(tokens, tokens, weight, weight, weight, slots, slots, slots),
        out_specs=(tokens, tokens, grad, grad, grad),
        check_vma=False,
    )
```

```python
import functools

import jax
import jax.numpy as jnp
from jax import lax
from jax.experimental import pallas as pl
from jax.experimental.pallas import tpu as pltpu
from jax.sharding import Mesh
from jax.sharding import PartitionSpec as P

BF16 = jnp.bfloat16
F32 = jnp.float32
XS, YS, CORES, RING = 4, 2, 2, 8
CHIPS = XS * YS
FIRST, LAST = 640, 768
VMEM_LIMIT = 40 * 1024 * 1024
FETCH_LIMIT = 60 * 1024 * 1024
WHOLE = pl.BlockSpec(memory_space=pltpu.VMEM)
SCALARS = pl.BlockSpec(memory_space=pltpu.SMEM)


def dot(left, right, left_dim, right_dim):
    return lax.dot_general(
        left, right, (((left_dim,), (right_dim,)), ((), ())), preferred_element_type=F32
    )


def core_swap(x):
    return lax.ppermute(x, "core", [(0, 1), (1, 0)])


def among_chips(x):
    return lax.all_to_all(x, ("x", "y"), 0, 0, tiled=True)


def along_y(x):
    return lax.ppermute(x, "y", [(0, 1), (1, 0)])


def along_x(x, by):
    return lax.ppermute(x, "x", [(i, (i + by) % XS) for i in range(XS)])


def ring(x, by):
    return lax.ppermute(x, "tensor", [(z, (z + by) % RING) for z in range(RING)])


def fetched(x):
    return pl.BlockSpec(x.shape, lambda i: (0,) * x.ndim)


def local_call(body, name, out_shape, operands, scratch=(), fetch=False):
    return pl.pallas_call(
        body,
        out_shape=out_shape,
        grid=(1,) if fetch else (),
        in_specs=[SCALARS] + [fetched(x) if fetch else WHOLE for x in operands[1:]],
        out_specs=jax.tree.map(lambda _: WHOLE, out_shape),
        scratch_shapes=scratch,
        compiler_params=pltpu.CompilerParams(
            vmem_limit_bytes=FETCH_LIMIT if fetch else VMEM_LIMIT
        ),
        cost_estimate=pl.CostEstimate(flops=1, bytes_accessed=1, transcendentals=0),
        name=name,
    )(*operands)


def column(row):
    size = row.shape[1]
    same = lax.broadcasted_iota(jnp.int32, (size, size), 0) == lax.broadcasted_iota(
        jnp.int32, (size, size), 1
    )
    return jnp.sum(jnp.where(same, row, 0.0), axis=1, keepdims=True)


def routes(count_ref, index_ref, gate_ref, token_count):
    size = index_ref.shape[1]
    live = lax.broadcasted_iota(jnp.int32, (1, size), 1) < count_ref[0]
    token = lax.broadcasted_iota(jnp.int32, (token_count, size), 0)
    place = jnp.where(token == index_ref[...], 1.0, 0.0).astype(BF16)
    weight = column(jnp.where(live, gate_ref[...], 0.0))
    return place, weight, column(jnp.where(live, 1.0, 0.0))


def gather_body(count_ref, tokens_ref, grads_ref, index_ref, gate_ref, out_ref):
    token_count, width = tokens_ref.shape
    place, weight, _ = routes(count_ref, index_ref, gate_ref, token_count)
    rows = dot(place, tokens_ref[...], 0, 0).astype(BF16)
    grads = (weight * dot(place, grads_ref[...], 0, 0)).astype(BF16)
    for n in range(CHIPS):
        out_ref[n, :, :width] = rows
        out_ref[n, :, width:] = grads


def pre_body(deltas, where_ref, rows_ref, w_rows_ref, w_grads_ref, payload_ref, *refs):
    here = where_ref[0]
    size = rows_ref.shape[1]
    width = rows_ref.shape[2] // 2
    for n, delta in enumerate(deltas):
        payload_ref[n * size : (n + 1) * size, :] = rows_ref[lax.rem(here + delta, RING)]
    by_rows = dot(payload_ref[:, :width], w_rows_ref[...], 1, 1)
    by_grads = dot(payload_ref[:, width:], w_grads_ref[...], 1, 1)
    mixed = by_rows[:, FIRST:] + by_grads[:, : LAST - FIRST]
    for n, ref in enumerate(refs):
        rows, kind = slice(n * size, (n + 1) * size), ref.dtype
        ref[:, :FIRST] = by_rows[rows, :FIRST].astype(kind)
        ref[:, FIRST:LAST] = mixed[rows].astype(kind)
        ref[:, LAST:] = by_grads[rows, LAST - FIRST :].astype(kind)


def join(refs, to_ref):
    size = refs[0].shape[0]
    for n, ref in enumerate(refs):
        to_ref[n * size : (n + 1) * size, :] = ref[...]


def out_body(where_ref, w_rows_ref, w_grads_ref, *refs):
    keep_ref, give_ref, acts_ref = refs[-3:]
    join(refs[:-3], acts_ref)
    size, width = keep_ref.shape[0], w_rows_ref.shape[1]
    out = dot(acts_ref[:, FIRST:], w_grads_ref[...], 1, 0)
    back = dot(acts_ref[:, :LAST], w_rows_ref[...], 1, 0)
    keep_ref[:, :width] = out[:size]
    keep_ref[:, width:] = back[:size]
    give_ref[:, :width] = out[size:].astype(BF16)
    give_ref[:, width:] = back[size:].astype(BF16)


def weight_body(block, where_ref, *refs):
    dp = where_ref[1]
    payload_refs = refs[:4]
    keep_ref, give_ref, acts_ref = refs[-3:]
    join(refs[4:-3], acts_ref)
    part = keep_ref.shape[0]
    width = 2 * part

    def product(cols, units):
        total, at = None, 0
        for ref in payload_refs:
            term = dot(ref[:, cols], acts_ref[at : at + ref.shape[0], units], 0, 0)
            total = term if total is None else total + term
            at += ref.shape[0]
        return total

    by_rows = product(slice(0, width), slice(0, LAST))
    by_grads = product(slice(width, 2 * width), slice(FIRST, acts_ref.shape[1]))
    unit = FIRST + lax.broadcasted_iota(jnp.int32, (part, LAST - FIRST), 1)
    for cols in (slice(0, FIRST), slice(FIRST, LAST), slice(LAST, acts_ref.shape[1])):
        halves = []
        for rows in (slice(0, part), slice(part, width)):
            if cols.stop == FIRST:
                halves.append(by_rows[rows, :FIRST])
            elif cols.start == FIRST:
                halves.append(
                    jnp.where(
                        unit < 2 * block, by_rows[rows, FIRST:], by_grads[rows, : LAST - FIRST]
                    )
                )
            else:
                halves.append(by_grads[rows, LAST - FIRST :])
        keep_ref[:, cols] = jnp.where(dp == 0, halves[0], halves[1])
        give_ref[:, cols] = jnp.where(dp == 0, halves[1], halves[0]).astype(BF16)


def pair_body(deltas, where_ref, keep_ref, keep_last_ref, got_ref, out_ref):
    here, x, y = where_ref[0], where_ref[2], where_ref[3]
    size = out_ref.shape[2]

    def place(delta):
        chip = lax.rem(here + delta, RING)
        along = lax.rem(lax.div(chip, YS) - x + XS, XS)
        return lax.rem(lax.rem(chip, YS) + y, YS), along

    for n, delta in enumerate(deltas):
        rows = slice(n * size, (n + 1) * size)
        out_ref[place(delta)] = (
            keep_ref[rows] + got_ref[rows].astype(F32)
        ).astype(BF16)
    out_ref[place(RING // 2)] = (
        keep_last_ref[...] + got_ref[len(deltas) * size :].astype(F32)
    ).astype(BF16)


def add(refs):
    total = refs[0][...].astype(F32)
    for ref in refs[1:]:
        total = total + ref[...].astype(F32)
    return total


def leave_body(where_ref, *refs):
    refs[-1][...] = add(refs[:-1]).astype(BF16)


def scatter_body(count_ref, *refs):
    index_ref, gate_ref, mixed_ref, grad_ref = refs[-4:]
    total = add(refs[:-4])
    token_count, width = mixed_ref.shape
    place, weight, live = routes(count_ref, index_ref, gate_ref, token_count)
    out_rows = (weight * total[:, :width]).astype(BF16)
    back_rows = jnp.where(live > 0.0, total[:, width:], 0.0).astype(BF16)
    mixed_ref[...] = dot(place, out_rows, 1, 0).astype(BF16)
    grad_ref[...] = dot(place, back_rows, 1, 0).astype(BF16)


def on_device(
    tokens, out_grad, gate_weight, up_weight, down_weight, route_count, route_index, route_gate
):
    capacity = route_index.shape[0]
    token_count, width = tokens.shape
    block = gate_weight.shape[0]
    units = 3 * block
    here = lax.axis_index("tensor")
    where = jnp.stack([here, lax.axis_index("dp"), lax.axis_index("x"), lax.axis_index("y")]).astype(jnp.int32)
    routing = [route_index[None, :], route_gate[None, :]]

    w_rows = jnp.concatenate(
        [gate_weight, up_weight, jnp.zeros((LAST - 2 * block, width), BF16)], axis=0
    )
    w_grads = jnp.concatenate(
        [jnp.zeros((2 * block - FIRST, width), BF16), down_weight], axis=0
    )

    copies = local_call(
        gather_body,
        "gather_rows",
        jax.ShapeDtypeStruct((CHIPS, capacity, 2 * width), BF16),
        [route_count, tokens, out_grad] + routing,
        fetch=True,
    )
    came = among_chips(copies)
    rows = [came, core_swap(came)]
    pre = {}
    payloads = []
    first, rest = (4, 3, 5), (2, 6, 1, 7, 0)
    for deltas, name in ((first, "pre_first"), (rest, "pre_rest")):
        for h in range(2):
            shapes = [jax.ShapeDtypeStruct((len(deltas) * capacity, 2 * width), BF16)]
            for delta in deltas:
                starts = delta == 4 or (delta, h) in ((3, 0), (5, 1))
                shapes.append(jax.ShapeDtypeStruct((capacity, units), BF16 if starts else F32))
            payload, *blocks = local_call(
                functools.partial(pre_body, deltas),
                name,
                shapes,
                [where, rows[h], w_rows, w_grads],
            )
            payloads.append(payload)
            pre.update({(delta, h): part for delta, part in zip(deltas, blocks)})
        if deltas is first:
            rows[0], payloads[1] = lax.optimization_barrier((rows[0], payloads[1]))

    own_left, own_right = ring(pre[4, 0], -1), ring(pre[3, 0], 1)
    own_left, own_right, payloads[1] = lax.optimization_barrier(
        (own_left, own_right, payloads[1])
    )
    sums = []
    for h, ways in (
        (0, ((own_left, (5, 6, 7), -1), (own_right, (2, 1), 1))),
        (1, ((None, (5, 6, 7), -1), (None, (4, 3, 2, 1), 1))),
    ):
        total = pre[0, h]
        for moving, path, by in ways:
            for delta in path:
                block_sum = pre[delta, h]
                if moving is not None:
                    block_sum = block_sum + moving.astype(F32)
                moving = ring(block_sum.astype(BF16), by)
            total = total + moving.astype(F32)
        sums.append(total)

    acts_own = []
    for total in sums:
        gate_pre, up_pre, d_hidden = (
            total[:, :block],
            total[:, block : 2 * block],
            total[:, 2 * block :],
        )
        sigmoid_gate = jax.nn.sigmoid(gate_pre)
        activated = gate_pre * sigmoid_gate
        hidden = (activated * up_pre).astype(BF16)
        d_gate = (
            d_hidden * up_pre * sigmoid_gate * (1.0 + gate_pre * (1.0 - sigmoid_gate))
        ).astype(BF16)
        d_up = (d_hidden * activated).astype(BF16)
        acts_own.append(jnp.concatenate([d_gate, d_up, hidden], axis=1))

    halves = {0: acts_own}
    right = list(acts_own)
    left = list(acts_own)
    for step in (1, 2, 3):
        right = [ring(a, 1) for a in right]
        left = [ring(a, -1) for a in left]
        halves[RING - step] = right
        halves[step] = left
    halves[4] = [ring(right[0], 1), ring(left[1], -1)]

    near, far = (0, 7, 1, 6, 2, 5, 3), (4,)
    kept, given = [], []
    for deltas, name in ((near, "out_near"), (far, "out_far")):
        shape = (len(deltas) * capacity, 2 * width)
        keep, give = local_call(
            out_body,
            name,
            [jax.ShapeDtypeStruct(shape, F32), jax.ShapeDtypeStruct(shape, BF16)],
            [where, w_rows, w_grads] + [halves[delta][h] for h in range(2) for delta in deltas],
            [pltpu.VMEM((2 * len(deltas) * capacity, units), BF16)],
        )
        kept.append(keep)
        given.append(give)
    swapped = core_swap(jnp.concatenate(given, axis=0))

    part = width // 2
    pieces = [halves[delta][h] for deltas in (first, rest) for h in range(2) for delta in deltas]
    keep_w, give_w = local_call(
        functools.partial(weight_body, block),
        "weight_grads",
        [jax.ShapeDtypeStruct((part, units), F32), jax.ShapeDtypeStruct((part, units), BF16)],
        [where] + payloads + pieces,
        [pltpu.VMEM((len(pieces) * capacity, units), BF16)],
    )
    swapped, give_w = lax.optimization_barrier((swapped, give_w))
    got_w = lax.ppermute(give_w, "dp", [(0, 1), (1, 0)])
    by_chip = local_call(
        functools.partial(pair_body, near),
        "pair_sum",
        jax.ShapeDtypeStruct((YS, XS, capacity, 2 * width), BF16),
        [where, kept[0], kept[1], swapped],
    )
    across = along_x(by_chip[:, 2], 2)
    leave = [across[1]] + [along_x(by_chip[1, by], by) for by in (1, 3)]
    stay = [across[0]] + [along_x(by_chip[0, by], by) for by in (1, 3)]
    gone = local_call(
        leave_body,
        "leave_sum",
        jax.ShapeDtypeStruct((capacity, 2 * width), BF16),
        [where, by_chip[1, 0]] + leave,
    )
    arrived = [by_chip[0, 0]] + stay + [along_y(gone)]
    mixed, input_grad = local_call(
        scatter_body,
        "scatter_rows",
        [jax.ShapeDtypeStruct((token_count, width), BF16)] * 2,
        [route_count, *arrived] + routing,
    )
    grads_w = keep_w + got_w.astype(F32)
    return (
        mixed,
        input_grad,
        grads_w[:, :block].T,
        grads_w[:, block : 2 * block].T,
        grads_w[:, 2 * block :].T,
    )


def solution(mesh):
    ways = (("x", "y", "core"), "tensor", "dp")
    chips = Mesh(mesh.devices.reshape(XS, YS, CORES, RING, 2), ways[0] + ways[1:])
    expert, tensor, dp = ways
    tokens = P(expert + (dp,), tensor)
    weight = P(expert, tensor)
    slots = P(expert + (dp,))
    grad = P(expert, (tensor, dp))
    return jax.shard_map(
        on_device,
        mesh=chips,
        in_specs=(tokens, tokens, weight, weight, weight, slots, slots, slots),
        out_specs=(tokens, tokens, grad, grad, grad),
        check_vma=False,
    )
```

```python
import functools

import jax
import jax.numpy as jnp
from jax import lax
from jax.experimental import pallas as pl
from jax.experimental.pallas import tpu as pltpu
from jax.sharding import Mesh
from jax.sharding import PartitionSpec as P

BF16 = jnp.bfloat16
F32 = jnp.float32
XS, YS, CORES, RING = 4, 2, 2, 8
CHIPS = XS * YS
FIRST, LAST = 640, 768
VMEM_LIMIT = 40 * 1024 * 1024
FETCH_LIMIT = 60 * 1024 * 1024
WHOLE = pl.BlockSpec(memory_space=pltpu.VMEM)
SCALARS = pl.BlockSpec(memory_space=pltpu.SMEM)


def dot(left, right, left_dim, right_dim):
    return lax.dot_general(
        left, right, (((left_dim,), (right_dim,)), ((), ())), preferred_element_type=F32
    )


def core_swap(x):
    return lax.ppermute(x, "core", [(0, 1), (1, 0)])


def among_chips(x):
    return lax.all_to_all(x, ("x", "y"), 0, 0, tiled=True)


def along_y(x):
    return lax.ppermute(x, "y", [(0, 1), (1, 0)])


def along_x(x, by):
    return lax.ppermute(x, "x", [(i, (i + by) % XS) for i in range(XS)])


def ring(x, by):
    return lax.ppermute(x, "tensor", [(z, (z + by) % RING) for z in range(RING)])


def fetched(x):
    return pl.BlockSpec(x.shape, lambda i: (0,) * x.ndim)


def local_call(body, name, out_shape, operands, scratch=(), fetch=False):
    return pl.pallas_call(
        body,
        out_shape=out_shape,
        grid=(1,) if fetch else (),
        in_specs=[SCALARS] + [fetched(x) if fetch else WHOLE for x in operands[1:]],
        out_specs=jax.tree.map(lambda _: WHOLE, out_shape),
        scratch_shapes=scratch,
        compiler_params=pltpu.CompilerParams(
            vmem_limit_bytes=FETCH_LIMIT if fetch else VMEM_LIMIT
        ),
        cost_estimate=pl.CostEstimate(flops=1, bytes_accessed=1, transcendentals=0),
        name=name,
    )(*operands)


def column(row):
    size = row.shape[1]
    same = lax.broadcasted_iota(jnp.int32, (size, size), 0) == lax.broadcasted_iota(
        jnp.int32, (size, size), 1
    )
    return jnp.sum(jnp.where(same, row, 0.0), axis=1, keepdims=True)


def routes(count_ref, index_ref, gate_ref, token_count):
    size = index_ref.shape[1]
    live = lax.broadcasted_iota(jnp.int32, (1, size), 1) < count_ref[0]
    token = lax.broadcasted_iota(jnp.int32, (token_count, size), 0)
    place = jnp.where(token == index_ref[...], 1.0, 0.0).astype(BF16)
    weight = column(jnp.where(live, gate_ref[...], 0.0))
    return place, weight, column(jnp.where(live, 1.0, 0.0))


def gather_body(count_ref, tokens_ref, grads_ref, index_ref, gate_ref, out_ref):
    token_count, width = tokens_ref.shape
    place, weight, _ = routes(count_ref, index_ref, gate_ref, token_count)
    rows = dot(place, tokens_ref[...], 0, 0).astype(BF16)
    grads = (weight * dot(place, grads_ref[...], 0, 0)).astype(BF16)
    for n in range(CHIPS):
        out_ref[n, :, :width] = rows
        out_ref[n, :, width:] = grads


def pre_body(deltas, where_ref, rows_ref, w_rows_ref, w_grads_ref, payload_ref, *refs):
    here = where_ref[0]
    size = rows_ref.shape[1]
    width = rows_ref.shape[2] // 2
    for n, delta in enumerate(deltas):
        payload_ref[n * size : (n + 1) * size, :] = rows_ref[lax.rem(here + delta, RING)]
    by_rows = dot(payload_ref[:, :width], w_rows_ref[...], 1, 1)
    by_grads = dot(payload_ref[:, width:], w_grads_ref[...], 1, 1)
    mixed = by_rows[:, FIRST:] + by_grads[:, : LAST - FIRST]
    for n, ref in enumerate(refs):
        rows, kind = slice(n * size, (n + 1) * size), ref.dtype
        ref[:, :FIRST] = by_rows[rows, :FIRST].astype(kind)
        ref[:, FIRST:LAST] = mixed[rows].astype(kind)
        ref[:, LAST:] = by_grads[rows, LAST - FIRST :].astype(kind)


def join(refs, to_ref):
    size = refs[0].shape[0]
    for n, ref in enumerate(refs):
        to_ref[n * size : (n + 1) * size, :] = ref[...]


def out_body(where_ref, w_rows_ref, w_grads_ref, *refs):
    keep_ref, give_ref, acts_ref = refs[-3:]
    join(refs[:-3], acts_ref)
    size, width = keep_ref.shape[0], w_rows_ref.shape[1]
    out = dot(acts_ref[:, FIRST:], w_grads_ref[...], 1, 0)
    back = dot(acts_ref[:, :LAST], w_rows_ref[...], 1, 0)
    keep_ref[:, :width] = out[:size]
    keep_ref[:, width:] = back[:size]
    give_ref[:, :width] = out[size:].astype(BF16)
    give_ref[:, width:] = back[size:].astype(BF16)


def weight_body(block, where_ref, *refs):
    dp = where_ref[1]
    payload_refs = refs[:4]
    keep_ref, give_ref, acts_ref = refs[-3:]
    join(refs[4:-3], acts_ref)
    part = keep_ref.shape[0]
    width = 2 * part

    def product(cols, units):
        total, at = None, 0
        for ref in payload_refs:
            term = dot(ref[:, cols], acts_ref[at : at + ref.shape[0], units], 0, 0)
            total = term if total is None else total + term
            at += ref.shape[0]
        return total

    by_rows = product(slice(0, width), slice(0, LAST))
    by_grads = product(slice(width, 2 * width), slice(FIRST, acts_ref.shape[1]))
    unit = FIRST + lax.broadcasted_iota(jnp.int32, (part, LAST - FIRST), 1)
    for cols in (slice(0, FIRST), slice(FIRST, LAST), slice(LAST, acts_ref.shape[1])):
        halves = []
        for rows in (slice(0, part), slice(part, width)):
            if cols.stop == FIRST:
                halves.append(by_rows[rows, :FIRST])
            elif cols.start == FIRST:
                halves.append(
                    jnp.where(
                        unit < 2 * block, by_rows[rows, FIRST:], by_grads[rows, : LAST - FIRST]
                    )
                )
            else:
                halves.append(by_grads[rows, LAST - FIRST :])
        keep_ref[:, cols] = jnp.where(dp == 0, halves[0], halves[1])
        give_ref[:, cols] = jnp.where(dp == 0, halves[1], halves[0]).astype(BF16)


def pair_body(deltas, where_ref, keep_ref, keep_last_ref, got_ref, out_ref):
    here, x, y = where_ref[0], where_ref[2], where_ref[3]
    size = out_ref.shape[2]

    def place(delta):
        chip = lax.rem(here + delta, RING)
        along = lax.rem(lax.div(chip, YS) - x + XS, XS)
        return lax.rem(lax.rem(chip, YS) + y, YS), along

    for n, delta in enumerate(deltas):
        rows = slice(n * size, (n + 1) * size)
        out_ref[place(delta)] = (
            keep_ref[rows] + got_ref[rows].astype(F32)
        ).astype(BF16)
    out_ref[place(RING // 2)] = (
        keep_last_ref[...] + got_ref[len(deltas) * size :].astype(F32)
    ).astype(BF16)


def add(refs):
    total = refs[0][...].astype(F32)
    for ref in refs[1:]:
        total = total + ref[...].astype(F32)
    return total


def leave_body(where_ref, *refs):
    refs[-1][...] = add(refs[:-1]).astype(BF16)


def scatter_body(count_ref, *refs):
    index_ref, gate_ref, mixed_ref, grad_ref = refs[-4:]
    total = add(refs[:-4])
    token_count, width = mixed_ref.shape
    place, weight, live = routes(count_ref, index_ref, gate_ref, token_count)
    out_rows = (weight * total[:, :width]).astype(BF16)
    back_rows = jnp.where(live > 0.0, total[:, width:], 0.0).astype(BF16)
    mixed_ref[...] = dot(place, out_rows, 1, 0).astype(BF16)
    grad_ref[...] = dot(place, back_rows, 1, 0).astype(BF16)


def on_device(
    tokens, out_grad, gate_weight, up_weight, down_weight, route_count, route_index, route_gate
):
    capacity = route_index.shape[0]
    token_count, width = tokens.shape
    block = gate_weight.shape[0]
    units = 3 * block
    here = lax.axis_index("tensor")
    where = jnp.stack([here, lax.axis_index("dp"), lax.axis_index("x"), lax.axis_index("y")]).astype(jnp.int32)
    routing = [route_index[None, :], route_gate[None, :]]

    w_rows = jnp.concatenate(
        [gate_weight, up_weight, jnp.zeros((LAST - 2 * block, width), BF16)], axis=0
    )
    w_grads = jnp.concatenate(
        [jnp.zeros((2 * block - FIRST, width), BF16), down_weight], axis=0
    )

    copies = local_call(
        gather_body,
        "gather_rows",
        jax.ShapeDtypeStruct((CHIPS, capacity, 2 * width), BF16),
        [route_count, tokens, out_grad] + routing,
        fetch=True,
    )
    came = among_chips(copies)
    rows = [came, core_swap(came)]
    pre = {}
    payloads = []
    first, rest = (4, 3, 5), (2, 6, 1, 7, 0)
    for deltas, name in ((first, "pre_first"), (rest, "pre_rest")):
        for h in range(2):
            shapes = [jax.ShapeDtypeStruct((len(deltas) * capacity, 2 * width), BF16)]
            for delta in deltas:
                starts = delta == 4 or (delta, h) in ((3, 0), (5, 1))
                shapes.append(jax.ShapeDtypeStruct((capacity, units), BF16 if starts else F32))
            payload, *blocks = local_call(
                functools.partial(pre_body, deltas),
                name,
                shapes,
                [where, rows[h], w_rows, w_grads],
            )
            payloads.append(payload)
            pre.update({(delta, h): part for delta, part in zip(deltas, blocks)})
        if deltas is first:
            rows[0], payloads[1] = lax.optimization_barrier((rows[0], payloads[1]))

    own_left, own_right = ring(pre[4, 0], -1), ring(pre[3, 0], 1)
    own_left, own_right, payloads[1] = lax.optimization_barrier(
        (own_left, own_right, payloads[1])
    )
    sums = []
    for h, ways in (
        (0, ((own_left, (5, 6, 7), -1), (own_right, (2, 1), 1))),
        (1, ((None, (5, 6, 7), -1), (None, (4, 3, 2, 1), 1))),
    ):
        total = pre[0, h]
        for moving, path, by in ways:
            for delta in path:
                block_sum = pre[delta, h]
                if moving is not None:
                    block_sum = block_sum + moving.astype(F32)
                moving = ring(block_sum.astype(BF16), by)
            total = total + moving.astype(F32)
        sums.append(total)

    acts_own = []
    for total in sums:
        gate_pre, up_pre, d_hidden = (
            total[:, :block],
            total[:, block : 2 * block],
            total[:, 2 * block :],
        )
        sigmoid_gate = jax.nn.sigmoid(gate_pre)
        activated = gate_pre * sigmoid_gate
        hidden = (activated * up_pre).astype(BF16)
        d_gate = (
            d_hidden * up_pre * sigmoid_gate * (1.0 + gate_pre * (1.0 - sigmoid_gate))
        ).astype(BF16)
        d_up = (d_hidden * activated).astype(BF16)
        acts_own.append(jnp.concatenate([d_gate, d_up, hidden], axis=1))

    halves = {0: acts_own}
    right = list(acts_own)
    left = list(acts_own)
    for step in (1, 2, 3):
        right = [ring(a, 1) for a in right]
        left = [ring(a, -1) for a in left]
        if step == 1:
            right[0], left[0], acts_own[1] = lax.optimization_barrier(
                (right[0], left[0], acts_own[1])
            )
        halves[RING - step] = right
        halves[step] = left
    halves[4] = [ring(right[0], 1), ring(left[1], -1)]

    near, far = (0, 7, 1, 6, 2, 5, 3), (4,)
    kept, given = [], []
    for deltas, name in ((near, "out_near"), (far, "out_far")):
        shape = (len(deltas) * capacity, 2 * width)
        keep, give = local_call(
            out_body,
            name,
            [jax.ShapeDtypeStruct(shape, F32), jax.ShapeDtypeStruct(shape, BF16)],
            [where, w_rows, w_grads] + [halves[delta][h] for h in range(2) for delta in deltas],
            [pltpu.VMEM((2 * len(deltas) * capacity, units), BF16)],
        )
        kept.append(keep)
        given.append(give)
    swapped = core_swap(jnp.concatenate(given, axis=0))

    part = width // 2
    pieces = [halves[delta][h] for deltas in (first, rest) for h in range(2) for delta in deltas]
    keep_w, give_w = local_call(
        functools.partial(weight_body, block),
        "weight_grads",
        [jax.ShapeDtypeStruct((part, units), F32), jax.ShapeDtypeStruct((part, units), BF16)],
        [where] + payloads + pieces,
        [pltpu.VMEM((len(pieces) * capacity, units), BF16)],
    )
    swapped, give_w = lax.optimization_barrier((swapped, give_w))
    got_w = lax.ppermute(give_w, "dp", [(0, 1), (1, 0)])
    by_chip = local_call(
        functools.partial(pair_body, near),
        "pair_sum",
        jax.ShapeDtypeStruct((YS, XS, capacity, 2 * width), BF16),
        [where, kept[0], kept[1], swapped],
    )
    across = along_x(by_chip[:, 2], 2)
    leave = [across[1]] + [along_x(by_chip[1, by], by) for by in (1, 3)]
    stay = [across[0]] + [along_x(by_chip[0, by], by) for by in (1, 3)]
    gone = local_call(
        leave_body,
        "leave_sum",
        jax.ShapeDtypeStruct((capacity, 2 * width), BF16),
        [where, by_chip[1, 0]] + leave,
    )
    arrived = [by_chip[0, 0]] + stay + [along_y(gone)]
    grads_w = (keep_w + got_w.astype(F32)).T
    grads = (grads_w[:block], grads_w[block : 2 * block], grads_w[2 * block :])
    arrived[0], *grads = lax.optimization_barrier((arrived[0], *grads))
    mixed, input_grad = local_call(
        scatter_body,
        "scatter_rows",
        [jax.ShapeDtypeStruct((token_count, width), BF16)] * 2,
        [route_count, *arrived] + routing,
    )
    return (mixed, input_grad, *grads)


def solution(mesh):
    ways = (("x", "y", "core"), "tensor", "dp")
    chips = Mesh(mesh.devices.reshape(XS, YS, CORES, RING, 2), ways[0] + ways[1:])
    expert, tensor, dp = ways
    tokens = P(expert + (dp,), tensor)
    weight = P(expert, tensor)
    slots = P(expert + (dp,))
    grad = P(expert, (tensor, dp))
    return jax.shard_map(
        on_device,
        mesh=chips,
        in_specs=(tokens, tokens, weight, weight, weight, slots, slots, slots),
        out_specs=(tokens, tokens, grad, grad, grad),
        check_vma=False,
    )
```
